32 devices in a mesh: gx: 4 (over z), gy: 2 (over x), gz: 4 (over y, core).
Axes of the slice: x: 2, y: 2, z: 4, core: 2. Of those that a mesh axis runs over, the one named last changes fastest.
Arguments:
- start_block: bfloat16 [24, 12, 96, 128], P('gx', 'gy', 'gz'), may hold values from -60 to 60
- locked_orbitals: bfloat16 [24, 12, 96, 384], P('gx', 'gy', 'gz'), may hold values from -5 to 5
- cell_h: bfloat16 [4, 2, 16, 343, 343], P('gx', 'gy', 'gz'), may hold values from -1 to 4, as said below
Outputs:
- orbitals: float32 [24, 12, 96, 128], P('gx', 'gy', 'gz')
The draws below stay inside these ranges and needn't reach their ends.
Inputs may be any that keep to these rules, and one draw needn't show every extreme that they name: `cell_h`: every cell matrix is symmetric.
All inputs are finite; a program needn't handle non-finite values.
Results may differ from the reference program's by a relative error of at most 0.0042.
Values may be sent and summed in bfloat16 or wider, within the bound.
A program may use at most 64 MiB of HBM per device.

```python
import math
import jax
import jax.numpy as jnp
from jax import lax

ORDER = 6
NODE = 343
APPLY = 6
BLOCK = 128
LOCKED = 384
CELLS_X = 4
CELLS_Y = 2
CELLS_Z = 16
NGX = 24
NGY = 12
NGZ = 96
NODES_ALL = 27648


def locked_draw(key):
    values = jax.random.normal(jax.random.fold_in(key, 11), (NGX, NGY, NGZ, LOCKED), jnp.float32)
    return jnp.clip(values, -5.0, 5.0)


def draw_locked_orbitals(key, part):
    return locked_draw(key).astype(jnp.bfloat16)


def draw_start_block(key, part):
    locked = locked_draw(key)
    mixing = jax.random.normal(jax.random.fold_in(key, 12), (LOCKED, BLOCK), jnp.float32) / math.sqrt(LOCKED)
    signal = jnp.dot(locked.reshape(-1, LOCKED), mixing).reshape(NGX, NGY, NGZ, BLOCK)
    noise = jax.random.normal(jax.random.fold_in(key, 13), (NGX, NGY, NGZ, BLOCK), jnp.float32)
    row_scale = jnp.exp(jax.random.uniform(jax.random.fold_in(key, 14), (NGX, NGY, NGZ, 1), jnp.float32, math.log(0.3), math.log(3.0)))
    column_scale = jnp.exp(jax.random.uniform(jax.random.fold_in(key, 15), (BLOCK,), jnp.float32, math.log(0.5), math.log(5.0)))
    values = row_scale * column_scale * (signal + noise) * 0.7071
    return jnp.clip(values, -60.0, 60.0).astype(jnp.bfloat16)


def draw_cell_h(key, part):
    base_key = jax.random.fold_in(key, 21)

    def slab(slab_index):
        slab_key = jax.random.fold_in(base_key, slab_index)
        diagonal = jax.random.uniform(jax.random.fold_in(slab_key, 1), (CELLS_Y, CELLS_Z, NODE), jnp.float32, 1.0, 3.0)
        off_diagonal = jax.random.uniform(jax.random.fold_in(slab_key, 2), (CELLS_Y, CELLS_Z, NODE, NODE), jnp.float32, -1.0, 1.0)
        symmetric = (off_diagonal + jnp.swapaxes(off_diagonal, 2, 3)) * (0.5 / math.sqrt(NODE))
        identity = jnp.eye(NODE, dtype=jnp.float32)
        return (symmetric + diagonal[..., None] * identity).astype(jnp.bfloat16)
    return lax.map(slab, jnp.arange(CELLS_X))


def setup_inputs(seed: int = 0) -> dict:
    keys = jax.random.split(jax.random.key(seed), 4)
    return {
        "start_block": draw_start_block(jax.random.fold_in(keys[3], 71), 0),
        "locked_orbitals": draw_locked_orbitals(jax.random.fold_in(keys[3], 71), 0),
        "cell_h": draw_cell_h(jax.random.fold_in(keys[3], 71), 0),
    }


filter_low = 3.0
filter_high = 40.0
filter_bottom = 0.5

def split_cells(grown, axis_pos, cell_count):
    head_part = lax.slice_in_dim(grown, 0, ORDER * cell_count, axis=axis_pos)
    head_part = head_part.reshape(grown.shape[:axis_pos] + (cell_count, ORDER) + grown.shape[axis_pos + 1:])
    tail_part = lax.slice_in_dim(grown, ORDER, ORDER * cell_count + 1, stride=ORDER, axis=axis_pos)
    tail_part = jnp.expand_dims(tail_part, axis_pos + 1)
    return jnp.concatenate([head_part, tail_part], axis_pos + 1)

def merge_cells(cell_local, axis_pos, cell_count):
    new_shape = cell_local.shape[:axis_pos] + (cell_count * ORDER,) + cell_local.shape[axis_pos + 2:]
    head_part = lax.slice_in_dim(cell_local, 0, ORDER, axis=axis_pos + 1).reshape(new_shape)
    tail_part = lax.slice_in_dim(cell_local, ORDER, ORDER + 1, axis=axis_pos + 1)
    zero_tail = jnp.zeros(cell_local.shape[:axis_pos + 1] + (ORDER - 1,) + cell_local.shape[axis_pos + 2:], cell_local.dtype)
    tail_part = jnp.concatenate([zero_tail, tail_part], axis_pos + 1).reshape(new_shape)
    zero_layer = jnp.zeros(cell_local.shape[:axis_pos] + (1,) + cell_local.shape[axis_pos + 2:], cell_local.dtype)
    return jnp.concatenate([head_part, zero_layer], axis_pos) + jnp.concatenate([zero_layer, tail_part], axis_pos)

def cell_terms(grown, cell_h):
    count_x, count_y, count_z = (cell_h.shape[0], cell_h.shape[1], cell_h.shape[2])
    block_width = grown.shape[3]
    cell_local = split_cells(grown, 0, count_x)
    cell_local = split_cells(cell_local, 2, count_y)
    cell_local = split_cells(cell_local, 4, count_z)
    cell_local = cell_local.transpose(0, 2, 4, 1, 3, 5, 6).reshape(count_x, count_y, count_z, NODE, block_width)
    products = lax.map(lambda operands: jnp.einsum('bcij,bcjv->bciv', operands[0].astype(jnp.float32), operands[1].astype(jnp.float32)), (cell_h, cell_local))
    side = ORDER + 1
    products = products.reshape(count_x, count_y, count_z, side, side, side, block_width).transpose(0, 3, 1, 4, 2, 5, 6)
    products = merge_cells(products, 4, count_z)
    products = merge_cells(products, 2, count_y)
    return merge_cells(products, 0, count_x)

def wrap_extend(values, axis_pos):
    return jnp.concatenate([values, lax.slice_in_dim(values, 0, 1, axis=axis_pos)], axis_pos)

def wrap_fold(values, axis_pos):
    total = values.shape[axis_pos]
    main_part = lax.slice_in_dim(values, 0, total - 1, axis=axis_pos)
    extra = lax.slice_in_dim(values, total - 1, total, axis=axis_pos)
    first_row = lax.slice_in_dim(main_part, 0, 1, axis=axis_pos) + extra
    return jnp.concatenate([first_row, lax.slice_in_dim(main_part, 1, total - 1, axis=axis_pos)], axis_pos)

def apply_operator(values, cell_h):
    grown = values.astype(jnp.bfloat16)
    grown = wrap_extend(wrap_extend(wrap_extend(grown, 0), 1), 2)
    terms = cell_terms(grown, cell_h)
    return wrap_fold(wrap_fold(wrap_fold(terms, 0), 1), 2)

def normalize(gram_matrix, vectors):
    factor = jnp.linalg.cholesky(gram_matrix)
    inverse = jax.scipy.linalg.solve_triangular(factor, jnp.eye(gram_matrix.shape[0], dtype=jnp.float32), lower=True)
    return jnp.dot(vectors.astype(jnp.float32), inverse.T.astype(jnp.float32), precision=lax.Precision.HIGHEST, preferred_element_type=jnp.float32)

def reference(start_block, locked_orbitals, cell_h):
    half_span = (filter_high - filter_low) / 2.0
    center = (filter_high + filter_low) / 2.0
    sigma_first = half_span / (filter_bottom - center)
    previous = start_block.astype(jnp.float32)
    current = sigma_first / half_span * (apply_operator(start_block, cell_h) - center * previous)
    sigma_now = sigma_first
    for repeat in range(APPLY - 1):
        sigma_next = 1.0 / (2.0 / sigma_first - sigma_now)
        following = 2.0 * sigma_next / half_span * (apply_operator(current, cell_h) - center * current) - sigma_now * sigma_next * previous
        previous = current
        current = following
        sigma_now = sigma_next
    block_width = start_block.shape[3]
    filtered = current.astype(jnp.bfloat16).reshape(-1, block_width)
    locked_flat = locked_orbitals.reshape(-1, LOCKED)
    contract = (((0,), (0,)), ((), ()))
    nodes_total = float(NODES_ALL)
    cross = lax.dot_general(locked_flat.astype(jnp.float32), filtered.astype(jnp.float32), contract, preferred_element_type=jnp.float32)
    coefficient = (cross / nodes_total).astype(jnp.bfloat16)
    projected = filtered.astype(jnp.float32) - jnp.dot(locked_flat.astype(jnp.float32), coefficient.astype(jnp.float32), preferred_element_type=jnp.float32)
    gram_matrix = lax.dot_general(projected.astype(jnp.float32), projected.astype(jnp.float32), contract, precision=lax.Precision.HIGHEST, preferred_element_type=jnp.float32) / nodes_total
    result = normalize(gram_matrix, projected)
    return result.reshape(start_block.shape)
```

```python
import functools

import jax
import jax.numpy as jnp
import numpy as np
from jax import lax
from jax.experimental import pallas as pl
from jax.experimental.pallas import tpu as pltpu
from jax.sharding import PartitionSpec as P

ORDER = 6
SIDE = ORDER + 1
TILE = 8
LINES = SIDE * SIDE
CELL_ROWS = LINES * TILE
APPLY = 6
AXES = ("gx", "gy", "gz")

filter_low = 3.0
filter_high = 40.0
filter_bottom = 0.5

MESH = pl.DeviceIdType.MESH
HIGHEST = lax.Precision.HIGHEST

Z_STEPS = ((0, 0, 1), (0, 0, -1))
X_STEPS = ((1, 0, 0), (-1, 0, 0))
Y_STEPS = ((0, 1, 0), (0, -1, 0))
XY_STEPS = ((1, 1, 0), (1, -1, 0), (-1, 1, 0), (-1, -1, 0))


def recurrence():
    half = (filter_high - filter_low) / 2.0
    center = (filter_high + filter_low) / 2.0
    first = half / (filter_bottom - center)
    rows = [(first / half, center, 0.0)]
    now = first
    for _ in range(APPLY - 1):
        later = 1.0 / (2.0 / first - now)
        rows.append((2.0 * later / half, center, now * later))
        now = later
    return np.asarray(rows, np.float32)


def side_of(step):
    return ORDER if step > 0 else 0


def dot_rows(a, b, precision=None):
    return lax.dot_general(
        a, b, (((0,), (0,)), ((), ())), precision=precision, preferred_element_type=jnp.float32
    )


def groups(sizes, rows):
    for scattered in (("gy", "gz"), ("gz",)):
        count = int(np.prod([sizes[a] for a in scattered]))
        if rows % (16 * count) == 0:
            return scattered, tuple(a for a in AXES if a not in scattered)
    return (), AXES


def count_of(sizes, axes):
    return int(np.prod([sizes[a] for a in axes], dtype=np.int64))


def index_in(sizes, axes):
    index = 0
    for axis in axes:
        index = index * sizes[axis] + lax.axis_index(axis)
    return index


def device_at(sizes, axes, index):
    place = {axis: lax.axis_index(axis) for axis in AXES}
    for axis in reversed(axes):
        place[axis] = lax.rem(index, sizes[axis])
        index = index // sizes[axis]
    return tuple(place[axis] for axis in AXES)


def neighbour(sizes, step):
    return tuple(
        lax.rem(lax.axis_index(axis) + d + sizes[axis], sizes[axis]) for axis, d in zip(AXES, step)
    )


def greeted(sizes, all_axes):
    steps = {
        tuple(d % sizes[a] for a, d in zip(AXES, step))
        for step in Z_STEPS + X_STEPS + Y_STEPS + XY_STEPS
    }
    for axes in all_axes:
        for place in np.ndindex(*[sizes[a] for a in axes]):
            near = dict(zip(axes, place))
            steps.add(tuple(int(near.get(a, 0)) for a in AXES))
    steps.discard((0, 0, 0))
    return sorted(steps)


def exchange(sizes, axes, source, slots, send_sem, recv_sem):
    count = count_of(sizes, axes)
    me = index_in(sizes, axes)
    copies = []
    for r in range(1, count):
        place = lax.rem(me + r, count)
        copies.append(
            pltpu.make_async_remote_copy(
                src_ref=source(place),
                dst_ref=slots.at[me],
                send_sem=send_sem.at[r - 1],
                recv_sem=recv_sem.at[r - 1],
                device_id=device_at(sizes, axes, place),
                device_id_type=MESH,
            )
        )
    for copy in copies:
        copy.start()
    for copy in copies:
        copy.wait()


def sum_over_devices(sizes, part, scratch, finish, gathered):
    scattered, whole = groups(sizes, part.shape[0])
    if scattered:
        slots, send_sem, recv_sem = scratch[0]
        chunk = slots.shape[1]
        me = index_in(sizes, scattered)
        rows = lambda place: part.at[pl.ds(pl.multiple_of(place * chunk, chunk), chunk)]
        slots[me] = rows(me)[...]
        exchange(sizes, scattered, rows, slots, send_sem, recv_sem)
        total = jnp.sum(slots[...], axis=0)
    else:
        me = 0
        total = part[...]
    for axis, (slots, send_sem, recv_sem) in zip(whole, scratch[1:-1]):
        place = lax.axis_index(axis)
        slots[place] = total
        exchange(sizes, (axis,), lambda _: slots.at[place], slots, send_sem, recv_sem)
        total = jnp.sum(slots[...], axis=0)
    gathered[me] = finish(total)
    if scattered:
        send_sem, recv_sem = scratch[-1]
        exchange(sizes, scattered, lambda _: gathered.at[me], gathered, send_sem, recv_sem)


def sum_scratch(sizes, rows, width):
    scattered, whole = groups(sizes, rows)
    count = count_of(sizes, scattered)
    chunk = rows // count
    sems = lambda n: [pltpu.SemaphoreType.DMA((max(n - 1, 1),))] * 2
    shapes = [[pltpu.VMEM((count, chunk, width), jnp.float32)] + sems(count)]
    for axis in whole:
        n = sizes[axis]
        shapes.append([pltpu.VMEM((n, chunk, width), jnp.float32)] + sems(n))
    shapes.append(sems(count))
    return shapes


def halo_sum(sizes, slot, work, z_send, z_recv, f_send, f_recv, e_send, e_recv, sems, cells):
    send_sem, recv_sem = sems
    width = work.shape[1]

    def remote(number, step, source, target):
        return pltpu.make_async_remote_copy(
            src_ref=source,
            dst_ref=target,
            send_sem=send_sem.at[slot, number],
            recv_sem=recv_sem.at[slot, number],
            device_id=neighbour(sizes, step),
            device_id_type=MESH,
        )

    def z_rows(cell, c):
        return pl.ds(cell * CELL_ROWS + c, LINES, stride=TILE)

    top, bottom = z_rows(cells - 1, ORDER), z_rows(0, 0)
    z_send[slot, 0] = work[top, :]
    z_send[slot, 1] = work[bottom, :]
    z_copies = [
        remote(n, step, z_send.at[slot, n], z_recv.at[slot, n]) for n, step in enumerate(Z_STEPS)
    ]
    for copy in z_copies:
        copy.start()
    for cell in range(cells - 1):
        lower, upper = z_rows(cell, ORDER), z_rows(cell + 1, 0)
        both = work[lower, :] + work[upper, :]
        work[lower, :] = both
        work[upper, :] = both
    for copy in z_copies:
        copy.wait()
    work[bottom, :] = work[bottom, :] + z_recv[slot, 0]
    work[top, :] = work[top, :] + z_recv[slot, 1]

    def x_rows(cell, a):
        return pl.ds(cell * CELL_ROWS + a * SIDE * TILE, SIDE * TILE)

    def line(cell, a, b):
        return pl.ds(cell * CELL_ROWS + (a * SIDE + b) * TILE, TILE)

    copies = []
    number = len(Z_STEPS)
    for n, step in enumerate(X_STEPS):
        face = [work[x_rows(k, side_of(step[0])), :] for k in range(cells)]
        f_send[slot, n] = jnp.concatenate(face, 0).astype(f_send.dtype)
        copies.append(remote(number + n, step, f_send.at[slot, n], f_recv.at[slot, n]))
        copies[-1].start()
    for n, step in enumerate(Y_STEPS, len(X_STEPS)):
        b = side_of(step[1])
        face = [work[line(k, a, b), :] for k in range(cells) for a in range(SIDE)]
        f_send[slot, n] = jnp.concatenate(face, 0).astype(f_send.dtype)
        copies.append(remote(number + n, step, f_send.at[slot, n], f_recv.at[slot, n]))
        copies[-1].start()
    number += len(X_STEPS) + len(Y_STEPS)
    for n, step in enumerate(XY_STEPS):
        a, b = side_of(step[0]), side_of(step[1])
        edge = [work[line(k, a, b), :] for k in range(cells)]
        e_send[slot, n] = jnp.concatenate(edge, 0).astype(e_send.dtype)
        copies.append(remote(number + n, step, e_send.at[slot, n], e_recv.at[slot, n]))
        copies[-1].start()
    for copy in copies:
        copy.wait()
    for n, step in enumerate(X_STEPS):
        got = f_recv[slot, n].astype(jnp.float32).reshape(cells, SIDE * TILE, width)
        for k in range(cells):
            at = x_rows(k, side_of(-step[0]))
            work[at, :] = work[at, :] + got[k]
    for n, step in enumerate(Y_STEPS, len(X_STEPS)):
        got = f_recv[slot, n].astype(jnp.float32).reshape(cells, SIDE, TILE, width)
        for k in range(cells):
            for a in range(SIDE):
                at = line(k, a, side_of(-step[1]))
                work[at, :] = work[at, :] + got[k, a]
    for n, step in enumerate(XY_STEPS):
        got = e_recv[slot, n].astype(jnp.float32).reshape(cells, TILE, width)
        for k in range(cells):
            at = line(k, side_of(-step[0]), side_of(-step[1]))
            work[at, :] = work[at, :] + got[k]


def inverse_factor(gram, both, inverse):
    n = gram.shape[0]
    row = lax.broadcasted_iota(jnp.int32, (n, n), 0)
    col = lax.broadcasted_iota(jnp.int32, (n, n), 1)
    both[:, :n] = gram
    both[:, n:] = jnp.where(row == col, 1.0, 0.0).astype(jnp.float32)
    sub = lax.broadcasted_iota(jnp.int32, (TILE, n), 0)
    for start in range(0, n, TILE):
        left = both[start : start + TILE, :n]
        right = both[start : start + TILE, n:]
        cols = [
            jnp.broadcast_to(left[:, start + t : start + t + 1], (TILE, n)) for t in range(TILE)
        ]
        scale = jnp.zeros((TILE, n), jnp.float32)
        for s in range(TILE):
            pivot = jnp.broadcast_to(cols[s][s : s + 1, :], (TILE, n))
            scale = jnp.where(sub == s, lax.rsqrt(pivot), scale)
            if s + 1 < TILE:
                ratio = jnp.where(sub > s, cols[s] / pivot, 0.0)
                for t in range(s + 1, TILE):
                    cols[t] = cols[t] - ratio * cols[t][s : s + 1, :]
                left = left - ratio * left[s : s + 1, :]
                right = right - ratio * right[s : s + 1, :]
        left = left * scale
        right = right * scale
        inverse[start : start + TILE, :] = right
        if start + TILE < n:
            rows = jnp.concatenate([left, right], axis=1)
            both[...] = both[...] - dot_rows(left, rows, HIGHEST)


def kernel(
    sizes,
    cells,
    nodes_total,
    coef_ref,
    start_ref,
    locked_ref,
    h_ref,
    out_ref,
    padded_h,
    grid_nodes,
    state,
    work,
    z_send,
    z_recv,
    f_send,
    f_recv,
    e_send,
    e_recv,
    halo_sems,
    cross_part,
    cross_scratch,
    coefficient,
    gram_part,
    gram_scratch,
    gram_rows,
    both,
    inverse,
):
    width = work.shape[1]
    node = h_ref.shape[1]
    steps = greeted(sizes, [groups(sizes, locked_ref.shape[1])[0], groups(sizes, width)[0], *[(a,) for a in AXES]])
    barrier = pltpu.get_barrier_semaphore()
    for step in steps:
        pl.semaphore_signal(
            barrier, inc=1, device_id=neighbour(sizes, step), device_id_type=MESH
        )

    row = lax.broadcasted_iota(jnp.int32, (CELL_ROWS, node), 0)
    col = lax.broadcasted_iota(jnp.int32, (CELL_ROWS, node), 1)
    place = jnp.where(row % TILE < SIDE, row // TILE * SIDE + row % TILE, -1)
    spread = jnp.where(col == place, 1.0, 0.0).astype(jnp.bfloat16)
    for k in range(cells):
        tall = jnp.dot(spread, h_ref[k], preferred_element_type=jnp.float32).astype(jnp.bfloat16)
        padded_h[k] = lax.dot_general(
            tall, spread, (((1,), (1,)), ((), ())), preferred_element_type=jnp.float32
        ).astype(jnp.bfloat16)

    own = start_ref.shape[2]
    grid_nodes[...] = jnp.zeros_like(grid_nodes)
    grid_nodes[:, :, :own, :] = start_ref[...].astype(jnp.float32)
    work[...] = jnp.zeros_like(work)
    sub = lax.broadcasted_iota(jnp.int32, (ORDER, TILE, width), 1)
    for k in range(cells):
        for a in range(ORDER):
            values = grid_nodes[a, :, ORDER * k : ORDER * k + TILE, :]
            first = k * CELL_ROWS + a * SIDE * TILE
            work[first : first + ORDER * TILE, :] = jnp.where(sub < ORDER, values, 0.0).reshape(
                ORDER * TILE, width
            )
    pl.semaphore_wait(barrier, len(steps))
    halo = (work, z_send, z_recv, f_send, f_recv, e_send, e_recv, halo_sems, cells)
    halo_sum(sizes, 0, *halo)
    state[0] = work[...]
    state[1] = jnp.zeros(state.shape[1:], jnp.float32)

    def apply(t, carry):
        now, slot = lax.rem(t - 1, 2), lax.rem(t, 2)
        for k in range(cells):
            rows = pl.ds(k * CELL_ROWS, CELL_ROWS)
            values = state[now, rows, :].astype(jnp.bfloat16)
            work[rows, :] = jnp.dot(padded_h[k], values, preferred_element_type=jnp.float32)
        halo_sum(sizes, slot, *halo)
        scale, shift, back = coef_ref[t - 1, 0], coef_ref[t - 1, 1], coef_ref[t - 1, 2]
        for k in range(cells):
            rows = pl.ds(k * CELL_ROWS, CELL_ROWS)
            state[slot, rows, :] = (
                scale * (work[rows, :] - shift * state[now, rows, :]) - back * state[slot, rows, :]
            )
        return carry

    lax.fori_loop(1, APPLY + 1, apply, 0)
    last = APPLY % 2
    for k in range(cells):
        for a in range(ORDER):
            first = k * CELL_ROWS + a * SIDE * TILE
            grid_nodes[a, :, ORDER * k : ORDER * k + TILE, :] = state[
                last, first : first + ORDER * TILE, :
            ].reshape(ORDER, TILE, width)
    filtered = (
        grid_nodes[:, :, :own, :].reshape(ORDER * ORDER * own, width).astype(jnp.bfloat16)
    )
    cross_part[...] = dot_rows(locked_ref[...], filtered)
    sum_over_devices(
        sizes,
        cross_part,
        cross_scratch,
        lambda total: (total / nodes_total).astype(jnp.bfloat16),
        coefficient,
    )
    projected = filtered.astype(jnp.float32) - jnp.dot(
        locked_ref[...],
        coefficient[...].reshape(locked_ref.shape[1], width),
        preferred_element_type=jnp.float32,
    )
    out_ref[...] = projected
    gram_part[...] = dot_rows(projected, projected, HIGHEST)
    sum_over_devices(sizes, gram_part, gram_scratch, lambda total: total / nodes_total, gram_rows)
    inverse_factor(gram_rows[...].reshape(width, width), both, inverse)
    out_ref[...] = lax.dot_general(
        out_ref[...],
        inverse[...],
        (((1,), (1,)), ((), ())),
        precision=HIGHEST,
        preferred_element_type=jnp.float32,
    )


def per_device(sizes, start_block, locked_orbitals, cell_h):
    width = start_block.shape[3]
    locked = locked_orbitals.shape[3]
    own = start_block.shape[2]
    cells = cell_h.shape[2]
    assert cell_h.shape[:2] == (1, 1)
    nodes = ORDER * ORDER * own
    nodes_total = float(nodes * count_of(sizes, AXES))
    count = lambda rows: count_of(sizes, groups(sizes, rows)[0])
    face = cells * SIDE * TILE
    messages = len(Z_STEPS) + len(X_STEPS) + len(Y_STEPS) + len(XY_STEPS)
    vmem = pltpu.VMEM
    scratch = [
        vmem((cells, CELL_ROWS, CELL_ROWS), jnp.bfloat16),
        vmem((ORDER, ORDER, own + TILE, width), jnp.float32),
        vmem((2, cells * CELL_ROWS, width), jnp.float32),
        vmem((cells * CELL_ROWS, width), jnp.float32),
        vmem((2, 2, LINES, width), jnp.float32),
        vmem((2, 2, LINES, width), jnp.float32),
        vmem((2, 4, face, width), jnp.bfloat16),
        vmem((2, 4, face, width), jnp.bfloat16),
        vmem((2, 4, cells * TILE, width), jnp.bfloat16),
        vmem((2, 4, cells * TILE, width), jnp.bfloat16),
        [pltpu.SemaphoreType.DMA((2, messages))] * 2,
        vmem((locked, width), jnp.float32),
        sum_scratch(sizes, locked, width),
        vmem((count(locked), locked // count(locked), width), jnp.bfloat16),
        vmem((width, width), jnp.float32),
        sum_scratch(sizes, width, width),
        vmem((count(width), width // count(width), width), jnp.float32),
        vmem((width, 2 * width), jnp.float32),
        vmem((width, width), jnp.float32),
    ]
    result = pl.pallas_call(
        functools.partial(kernel, sizes, cells, nodes_total),
        out_shape=jax.ShapeDtypeStruct((nodes, width), jnp.float32),
        in_specs=[pl.BlockSpec(memory_space=pltpu.SMEM)]
        + [pl.BlockSpec(memory_space=pltpu.VMEM)] * 3,
        out_specs=pl.BlockSpec(memory_space=pltpu.VMEM),
        scratch_shapes=scratch,
        compiler_params=pltpu.CompilerParams(
            collective_id=0, has_side_effects=True, vmem_limit_bytes=40 << 20
        ),
    )(
        jnp.asarray(recurrence()),
        start_block,
        locked_orbitals.reshape(nodes, locked),
        cell_h.reshape(cell_h.shape[2:]),
    )
    return result.reshape(start_block.shape)


def solution(mesh):
    sizes = dict(mesh.shape)
    placed = (P("gx", "gy", "gz", None), P("gx", "gy", "gz", None), P("gx", "gy", "gz", None, None))
    return jax.shard_map(
        functools.partial(per_device, sizes),
        mesh=mesh,
        in_specs=placed,
        out_specs=P("gx", "gy", "gz", None),
        check_vma=False,
    )
```

```python
import functools

import jax
import jax.numpy as jnp
import numpy as np
from jax import lax
from jax.experimental import pallas as pl
from jax.experimental.pallas import tpu as pltpu
from jax.sharding import PartitionSpec as P

ORDER = 6
SIDE = ORDER + 1
TILE = 8
LINES = SIDE * SIDE
CELL_ROWS = LINES * TILE
APPLY = 6
BLOCK_ROWS = 16
AXES = ("gx", "gy", "gz")

filter_low = 3.0
filter_high = 40.0
filter_bottom = 0.5

MESH = pl.DeviceIdType.MESH
HIGHEST = lax.Precision.HIGHEST

Z_STEPS = ((0, 0, 1), (0, 0, -1))
X_STEPS = ((1, 0, 0), (-1, 0, 0))
Y_STEPS = ((0, 1, 0), (0, -1, 0))
XY_STEPS = ((1, 1, 0), (1, -1, 0), (-1, 1, 0), (-1, -1, 0))


def recurrence():
    half = (filter_high - filter_low) / 2.0
    center = (filter_high + filter_low) / 2.0
    first = half / (filter_bottom - center)
    rows = [(1.0, 0.0, 0.0), (first / half, center, 0.0)]
    now = first
    for _ in range(APPLY - 1):
        later = 1.0 / (2.0 / first - now)
        rows.append((2.0 * later / half, center, now * later))
        now = later
    return np.asarray(rows, np.float32)


def side_of(step):
    return ORDER if step > 0 else 0


def dot_rows(a, b, precision=None):
    return lax.dot_general(
        a, b, (((0,), (0,)), ((), ())), precision=precision, preferred_element_type=jnp.float32
    )


def groups(sizes, rows):
    for scattered in (("gy", "gz"), ("gz",)):
        count = int(np.prod([sizes[a] for a in scattered]))
        if rows % (16 * count) == 0:
            return scattered, tuple(a for a in AXES if a not in scattered)
    return (), AXES


def count_of(sizes, axes):
    return int(np.prod([sizes[a] for a in axes], dtype=np.int64))


def index_in(sizes, axes):
    index = 0
    for axis in axes:
        index = index * sizes[axis] + lax.axis_index(axis)
    return index


def device_at(sizes, axes, index):
    place = {axis: lax.axis_index(axis) for axis in AXES}
    for axis in reversed(axes):
        place[axis] = lax.rem(index, sizes[axis])
        index = index // sizes[axis]
    return tuple(place[axis] for axis in AXES)


def neighbour(sizes, step):
    return tuple(
        lax.rem(lax.axis_index(axis) + d + sizes[axis], sizes[axis]) for axis, d in zip(AXES, step)
    )


def greeted(sizes, all_axes):
    steps = {
        tuple(d % sizes[a] for a, d in zip(AXES, step))
        for step in Z_STEPS + X_STEPS + Y_STEPS + XY_STEPS
    }
    for axes in all_axes:
        for place in np.ndindex(*[sizes[a] for a in axes]):
            near = dict(zip(axes, place))
            steps.add(tuple(int(near.get(a, 0)) for a in AXES))
    steps.discard((0, 0, 0))
    return sorted(steps)


def exchange(sizes, axes, source, slots, send_sem, recv_sem):
    count = count_of(sizes, axes)
    me = index_in(sizes, axes)
    copies = []
    for r in range(1, count):
        place = lax.rem(me + r, count)
        copies.append(
            pltpu.make_async_remote_copy(
                src_ref=source(place),
                dst_ref=slots.at[me],
                send_sem=send_sem.at[r - 1],
                recv_sem=recv_sem.at[r - 1],
                device_id=device_at(sizes, axes, place),
                device_id_type=MESH,
            )
        )
    for copy in copies:
        copy.start()
    for copy in copies:
        copy.wait()


def sum_over_devices(sizes, part, scratch, finish, gathered):
    scattered, whole = groups(sizes, part.shape[0])
    if scattered:
        slots, send_sem, recv_sem = scratch[0]
        chunk = slots.shape[1]
        me = index_in(sizes, scattered)
        rows = lambda place: part.at[pl.ds(pl.multiple_of(place * chunk, chunk), chunk)]
        slots[me] = rows(me)[...]
        exchange(sizes, scattered, rows, slots, send_sem, recv_sem)
        total = jnp.sum(slots[...], axis=0)
    else:
        me = 0
        total = part[...]
    for axis, (slots, send_sem, recv_sem) in zip(whole, scratch[1:-1]):
        place = lax.axis_index(axis)
        slots[place] = total
        exchange(sizes, (axis,), lambda _: slots.at[place], slots, send_sem, recv_sem)
        total = jnp.sum(slots[...], axis=0)
    gathered[me] = finish(total)
    if scattered:
        send_sem, recv_sem = scratch[-1]
        exchange(sizes, scattered, lambda _: gathered.at[me], gathered, send_sem, recv_sem)


def sum_scratch(sizes, rows, width):
    scattered, whole = groups(sizes, rows)
    count = count_of(sizes, scattered)
    chunk = rows // count
    sems = lambda n: [pltpu.SemaphoreType.DMA((max(n - 1, 1),))] * 2
    shapes = [[pltpu.VMEM((count, chunk, width), jnp.float32)] + sems(count)]
    for axis in whole:
        n = sizes[axis]
        shapes.append([pltpu.VMEM((n, chunk, width), jnp.float32)] + sems(n))
    shapes.append(sems(count))
    return shapes


def merged(sizes):
    found = {}
    for step in X_STEPS + Y_STEPS + XY_STEPS:
        found.setdefault(tuple(d % sizes[a] for a, d in zip(AXES, step)), []).append(step)
    return list(found.values())


def part_rows(step, count):
    return count * TILE * (SIDE if 0 in step[:2] else 1)


class Halo:
    def __init__(self, sizes, cells, work, z_send, z_recv, f_send, f_recv, sems):
        self.sizes, self.cells, self.work = sizes, cells, work
        self.z_send, self.z_recv = z_send, z_recv
        self.f_send, self.f_recv = f_send, f_recv
        self.send_sem, self.recv_sem = sems
        self.messages = merged(sizes)

    def remote(self, slot, number, step, source, target):
        return pltpu.make_async_remote_copy(
            src_ref=source,
            dst_ref=target,
            send_sem=self.send_sem.at[slot, number],
            recv_sem=self.recv_sem.at[slot, number],
            device_id=neighbour(self.sizes, step),
            device_id_type=MESH,
        )

    def lines(self, cell, step):
        first = cell * CELL_ROWS
        if step[1] == 0:
            return [pl.ds(first + side_of(step[0]) * SIDE * TILE, SIDE * TILE)]
        if step[0] == 0:
            rows = range(SIDE)
        else:
            rows = [side_of(step[0])]
        return [pl.ds(first + (a * SIDE + side_of(step[1])) * TILE, TILE) for a in rows]

    def send_faces(self, slot, group, cells):
        copies = []
        row = 0
        for n, steps in enumerate(self.messages):
            begin = row
            for step in steps:
                part = [self.work[at, :] for k in cells for at in self.lines(k, step)]
                size = part_rows(step, len(cells))
                self.f_send[slot, group, row : row + size, :] = jnp.concatenate(part, 0).astype(
                    self.f_send.dtype
                )
                row += size
            rows = pl.ds(begin, row - begin)
            copies.append(
                self.remote(
                    slot,
                    len(Z_STEPS) + group * len(self.messages) + n,
                    steps[0],
                    self.f_send.at[slot, group, rows],
                    self.f_recv.at[slot, group, rows],
                )
            )
            copies[-1].start()
        return copies

    def add_faces(self, slot, group, cells, copies):
        row = 0
        for copy, steps in zip(copies, self.messages):
            copy.wait()
            for step in steps:
                size = part_rows(step, len(cells))
                got = self.f_recv[slot, group, row : row + size, :].astype(jnp.float32)
                row += size
                taken = 0
                for k in cells:
                    for at in self.lines(k, tuple(-d for d in step)):
                        self.work[at, :] = self.work[at, :] + got[taken : taken + at.size]
                        taken += at.size

    def z_rows(self, cell, c):
        return pl.ds(cell * CELL_ROWS + c, LINES, stride=TILE)

    def z_copies(self, slot):
        return [
            self.remote(slot, n, step, self.z_send.at[slot, n], self.z_recv.at[slot, n])
            for n, step in enumerate(Z_STEPS)
        ]

    def send_z(self, slot):
        work = self.work
        self.z_send[slot, 0] = work[self.z_rows(self.cells - 1, ORDER), :]
        self.z_send[slot, 1] = work[self.z_rows(0, 0), :]
        for copy in self.z_copies(slot):
            copy.start()
        for cell in range(self.cells - 1):
            lower, upper = self.z_rows(cell, ORDER), self.z_rows(cell + 1, 0)
            both = work[lower, :] + work[upper, :]
            work[lower, :] = both
            work[upper, :] = both

    def add_z(self, slot):
        work = self.work
        for copy in self.z_copies(slot):
            copy.wait()
        bottom, top = self.z_rows(0, 0), self.z_rows(self.cells - 1, ORDER)
        work[bottom, :] = work[bottom, :] + self.z_recv[slot, 0]
        work[top, :] = work[top, :] + self.z_recv[slot, 1]


def inverse_factor(gram, mixed, inverse):
    n = gram.shape[0]
    size = BLOCK_ROWS if n % BLOCK_ROWS == 0 else TILE
    mixed[...] = gram
    sub = lax.broadcasted_iota(jnp.int32, (size, n), 0)
    col = lax.broadcasted_iota(jnp.int32, (size, n), 1)
    for start in range(0, n, size):
        end = start + size
        rows = mixed[start:end, :]
        cols = [jnp.broadcast_to(rows[:, start + t : start + t + 1], (size, n)) for t in range(size)]
        unit = jnp.where(col - start == sub, 1.0, 0.0).astype(jnp.float32)
        rows = jnp.where((col >= start) & (col < end), unit, rows)
        scale = jnp.zeros((size, n), jnp.float32)
        for s in range(size):
            root = lax.rsqrt(cols[s][s : s + 1, :])
            scale = jnp.where(sub == s, root, scale)
            if s + 1 < size:
                ratio = jnp.where(sub > s, cols[s] * (root * root), 0.0)
                for t in range(s + 1, size):
                    cols[t] = cols[t] - ratio * cols[t][s : s + 1, :]
                rows = rows - ratio * rows[s : s + 1, :]
        rows = rows * scale
        inverse[start:end, :] = jnp.where(col < end, rows, 0.0)
        if end < n:
            change = dot_rows(jnp.where(col >= end, rows, 0.0), rows, HIGHEST)[end:, :]
            rest = lax.broadcasted_iota(jnp.int32, (n - end, n), 1)
            kept = jnp.where((rest >= start) & (rest < end), 0.0, mixed[end:, :])
            mixed[end:, :] = kept - change


def kernel(
    sizes,
    cells,
    nodes_total,
    coef_ref,
    start_ref,
    locked_ref,
    h_ref,
    out_ref,
    padded_h,
    grid_nodes,
    state,
    work,
    z_send,
    z_recv,
    f_send,
    f_recv,
    halo_sems,
    cross_part,
    cross_scratch,
    coefficient,
    gram_part,
    gram_scratch,
    gram_rows,
    mixed,
    inverse,
):
    width = work.shape[1]
    node = h_ref.shape[1]
    steps = greeted(sizes, [groups(sizes, locked_ref.shape[1])[0], groups(sizes, width)[0], *[(a,) for a in AXES]])
    barrier = pltpu.get_barrier_semaphore()
    for step in steps:
        pl.semaphore_signal(
            barrier, inc=1, device_id=neighbour(sizes, step), device_id_type=MESH
        )

    row = lax.broadcasted_iota(jnp.int32, (CELL_ROWS, node), 0)
    col = lax.broadcasted_iota(jnp.int32, (CELL_ROWS, node), 1)
    place = jnp.where(row % TILE < SIDE, row // TILE * SIDE + row % TILE, -1)
    spread = jnp.where(col == place, 1.0, 0.0).astype(jnp.bfloat16)
    for k in range(cells):
        tall = jnp.dot(spread, h_ref[k], preferred_element_type=jnp.float32).astype(jnp.bfloat16)
        padded_h[k] = lax.dot_general(
            tall, spread, (((1,), (1,)), ((), ())), preferred_element_type=jnp.float32
        ).astype(jnp.bfloat16)

    own = start_ref.shape[2]
    grid_nodes[...] = jnp.zeros_like(grid_nodes)
    grid_nodes[:, :, :own, :] = start_ref[...].astype(jnp.float32)
    work[...] = jnp.zeros_like(work)
    sub = lax.broadcasted_iota(jnp.int32, (ORDER, TILE, width), 1)
    for k in range(cells):
        for a in range(ORDER):
            values = grid_nodes[a, :, ORDER * k : ORDER * k + TILE, :]
            first = k * CELL_ROWS + a * SIDE * TILE
            work[first : first + ORDER * TILE, :] = jnp.where(sub < ORDER, values, 0.0).reshape(
                ORDER * TILE, width
            )
    pl.semaphore_wait(barrier, len(steps))
    halo = Halo(sizes, cells, work, z_send, z_recv, f_send, f_recv, halo_sems)
    inner, outer = tuple(range(1, cells - 1)), (0, cells - 1)
    state[...] = jnp.zeros(state.shape, jnp.float32)

    def finish_faces(slot, inner_copies, outer_copies):
        halo.add_faces(slot, 0, inner, inner_copies)
        halo.add_faces(slot, 1, outer, outer_copies)
        halo.send_z(slot)

    def update(t, group):
        now, old = lax.rem(t, 2), lax.rem(t + 1, 2)
        scale, shift, back = coef_ref[t, 0], coef_ref[t, 1], coef_ref[t, 2]
        for k in group:
            rows = pl.ds(k * CELL_ROWS, CELL_ROWS)
            state[now, rows, :] = (
                scale * (work[rows, :] - shift * state[old, rows, :]) - back * state[now, rows, :]
            )

    def multiply(t, group):
        for k in group:
            rows = pl.ds(k * CELL_ROWS, CELL_ROWS)
            values = state[lax.rem(t, 2), rows, :].astype(jnp.bfloat16)
            work[rows, :] = jnp.dot(padded_h[k], values, preferred_element_type=jnp.float32)

    finish_faces(0, halo.send_faces(0, 0, inner), halo.send_faces(0, 1, outer))

    def apply(t, carry):
        slot = lax.rem(t, 2)
        update(t - 1, inner)
        multiply(t - 1, inner)
        inner_copies = halo.send_faces(slot, 0, inner)
        halo.add_z(lax.rem(t - 1, 2))
        update(t - 1, outer)
        multiply(t - 1, outer)
        outer_copies = halo.send_faces(slot, 1, outer)
        finish_faces(slot, inner_copies, outer_copies)
        return carry

    lax.fori_loop(1, APPLY + 1, apply, 0)
    update(APPLY, inner)
    halo.add_z(APPLY % 2)
    update(APPLY, outer)
    last = APPLY % 2
    for k in range(cells):
        for a in range(ORDER):
            first = k * CELL_ROWS + a * SIDE * TILE
            grid_nodes[a, :, ORDER * k : ORDER * k + TILE, :] = state[
                last, first : first + ORDER * TILE, :
            ].reshape(ORDER, TILE, width)
    filtered = (
        grid_nodes[:, :, :own, :].reshape(ORDER * ORDER * own, width).astype(jnp.bfloat16)
    )
    cross_part[...] = dot_rows(locked_ref[...], filtered)
    sum_over_devices(
        sizes,
        cross_part,
        cross_scratch,
        lambda total: (total / nodes_total).astype(jnp.bfloat16),
        coefficient,
    )
    projected = filtered.astype(jnp.float32) - jnp.dot(
        locked_ref[...],
        coefficient[...].reshape(locked_ref.shape[1], width),
        preferred_element_type=jnp.float32,
    )
    out_ref[...] = projected
    gram_part[...] = dot_rows(projected, projected, HIGHEST)
    sum_over_devices(sizes, gram_part, gram_scratch, lambda total: total / nodes_total, gram_rows)
    inverse_factor(gram_rows[...].reshape(width, width), mixed, inverse)
    out_ref[...] = lax.dot_general(
        out_ref[...],
        inverse[...],
        (((1,), (1,)), ((), ())),
        precision=HIGHEST,
        preferred_element_type=jnp.float32,
    )


def per_device(sizes, start_block, locked_orbitals, cell_h):
    width = start_block.shape[3]
    locked = locked_orbitals.shape[3]
    own = start_block.shape[2]
    cells = cell_h.shape[2]
    assert cell_h.shape[:2] == (1, 1)
    nodes = ORDER * ORDER * own
    nodes_total = float(nodes * count_of(sizes, AXES))
    count = lambda rows: count_of(sizes, groups(sizes, rows)[0])
    largest = max(cells - 2, 2)
    faces = sum(part_rows(step, largest) for step in X_STEPS + Y_STEPS + XY_STEPS)
    messages = len(Z_STEPS) + 2 * len(merged(sizes))
    vmem = pltpu.VMEM
    scratch = [
        vmem((cells, CELL_ROWS, CELL_ROWS), jnp.bfloat16),
        vmem((ORDER, ORDER, own + TILE, width), jnp.float32),
        vmem((2, cells * CELL_ROWS, width), jnp.float32),
        vmem((cells * CELL_ROWS, width), jnp.float32),
        vmem((2, 2, LINES, width), jnp.float32),
        vmem((2, 2, LINES, width), jnp.float32),
        vmem((2, 2, faces, width), jnp.bfloat16),
        vmem((2, 2, faces, width), jnp.bfloat16),
        [pltpu.SemaphoreType.DMA((2, messages))] * 2,
        vmem((locked, width), jnp.float32),
        sum_scratch(sizes, locked, width),
        vmem((count(locked), locked // count(locked), width), jnp.bfloat16),
        vmem((width, width), jnp.float32),
        sum_scratch(sizes, width, width),
        vmem((count(width), width // count(width), width), jnp.float32),
        vmem((width, width), jnp.float32),
        vmem((width, width), jnp.float32),
    ]
    result = pl.pallas_call(
        functools.partial(kernel, sizes, cells, nodes_total),
        out_shape=jax.ShapeDtypeStruct((nodes, width), jnp.float32),
        in_specs=[pl.BlockSpec(memory_space=pltpu.SMEM)]
        + [pl.BlockSpec(memory_space=pltpu.VMEM)] * 3,
        out_specs=pl.BlockSpec(memory_space=pltpu.VMEM),
        scratch_shapes=scratch,
        compiler_params=pltpu.CompilerParams(
            collective_id=0, has_side_effects=True, vmem_limit_bytes=40 << 20
        ),
    )(
        jnp.asarray(recurrence()),
        start_block,
        locked_orbitals.reshape(nodes, locked),
        cell_h.reshape(cell_h.shape[2:]),
    )
    return result.reshape(start_block.shape)


def solution(mesh):
    sizes = dict(mesh.shape)
    placed = (P("gx", "gy", "gz", None), P("gx", "gy", "gz", None), P("gx", "gy", "gz", None, None))
    return jax.shard_map(
        functools.partial(per_device, sizes),
        mesh=mesh,
        in_specs=placed,
        out_specs=P("gx", "gy", "gz", None),
        check_vma=False,
    )
```

```python
import functools

import jax
import jax.numpy as jnp
import numpy as np
from jax import lax
from jax.experimental import pallas as pl
from jax.experimental.pallas import tpu as pltpu
from jax.sharding import PartitionSpec as P

ORDER = 6
SIDE = ORDER + 1
TILE = 8
LINES = SIDE * SIDE
CELL_ROWS = LINES * TILE
APPLY = 6
BLOCK_ROWS = 16
AXES = ("gx", "gy", "gz")

filter_low = 3.0
filter_high = 40.0
filter_bottom = 0.5

MESH = pl.DeviceIdType.MESH
HIGHEST = lax.Precision.HIGHEST

Z_STEPS = ((0, 0, 1), (0, 0, -1))
X_STEPS = ((1, 0, 0), (-1, 0, 0))
Y_STEPS = ((0, 1, 0), (0, -1, 0))
XY_STEPS = ((1, 1, 0), (1, -1, 0), (-1, 1, 0), (-1, -1, 0))


def recurrence():
    half = (filter_high - filter_low) / 2.0
    center = (filter_high + filter_low) / 2.0
    first = half / (filter_bottom - center)
    rows = [(1.0, 0.0, 0.0), (first / half, center, 0.0)]
    now = first
    for _ in range(APPLY - 1):
        later = 1.0 / (2.0 / first - now)
        rows.append((2.0 * later / half, center, now * later))
        now = later
    return np.asarray(rows, np.float32)


def side_of(step):
    return ORDER if step > 0 else 0


def dot_rows(a, b, precision=None):
    return lax.dot_general(
        a, b, (((0,), (0,)), ((), ())), precision=precision, preferred_element_type=jnp.float32
    )


def split(values):
    high = values.astype(jnp.bfloat16)
    return high, (values - high.astype(jnp.float32)).astype(jnp.bfloat16)


def groups(sizes, rows):
    for scattered in (("gy", "gz"), ("gz",)):
        count = int(np.prod([sizes[a] for a in scattered]))
        if rows % (16 * count) == 0:
            return scattered, tuple(a for a in AXES if a not in scattered)
    return (), AXES


def count_of(sizes, axes):
    return int(np.prod([sizes[a] for a in axes], dtype=np.int64))


def index_in(sizes, axes):
    index = 0
    for axis in axes:
        index = index * sizes[axis] + lax.axis_index(axis)
    return index


def device_at(sizes, axes, index):
    place = {axis: lax.axis_index(axis) for axis in AXES}
    for axis in reversed(axes):
        place[axis] = lax.rem(index, sizes[axis])
        index = index // sizes[axis]
    return tuple(place[axis] for axis in AXES)


def neighbour(sizes, step):
    return tuple(
        lax.rem(lax.axis_index(axis) + d + sizes[axis], sizes[axis]) for axis, d in zip(AXES, step)
    )


def greeted(sizes, all_axes):
    steps = {
        tuple(d % sizes[a] for a, d in zip(AXES, step))
        for step in Z_STEPS + X_STEPS + Y_STEPS + XY_STEPS
    }
    for axes in all_axes:
        for place in np.ndindex(*[sizes[a] for a in axes]):
            near = dict(zip(axes, place))
            steps.add(tuple(int(near.get(a, 0)) for a in AXES))
    steps.discard((0, 0, 0))
    return sorted(steps)


def exchange(sizes, axes, source, slots, send_sem, recv_sem):
    count = count_of(sizes, axes)
    me = index_in(sizes, axes)
    copies = []
    for r in range(1, count):
        place = lax.rem(me + r, count)
        copies.append(
            pltpu.make_async_remote_copy(
                src_ref=source(place),
                dst_ref=slots.at[me],
                send_sem=send_sem.at[r - 1],
                recv_sem=recv_sem.at[r - 1],
                device_id=device_at(sizes, axes, place),
                device_id_type=MESH,
            )
        )
    for copy in copies:
        copy.start()
    for copy in copies:
        copy.wait()


def sum_over_devices(sizes, part, scratch, finish, gathered):
    scattered, whole = groups(sizes, part.shape[0])
    if scattered:
        slots, send_sem, recv_sem = scratch[0]
        chunk = slots.shape[1]
        me = index_in(sizes, scattered)
        rows = lambda place: part.at[pl.ds(pl.multiple_of(place * chunk, chunk), chunk)]
        slots[me] = rows(me)[...]
        exchange(sizes, scattered, rows, slots, send_sem, recv_sem)
        total = jnp.sum(slots[...], axis=0)
    else:
        me = 0
        total = part[...]
    for axis, (slots, send_sem, recv_sem) in zip(whole, scratch[1:-1]):
        place = lax.axis_index(axis)
        slots[place] = total
        exchange(sizes, (axis,), lambda _: slots.at[place], slots, send_sem, recv_sem)
        total = jnp.sum(slots[...], axis=0)
    gathered[me] = finish(total)
    if scattered:
        send_sem, recv_sem = scratch[-1]
        exchange(sizes, scattered, lambda _: gathered.at[me], gathered, send_sem, recv_sem)


def sum_scratch(sizes, rows, width):
    scattered, whole = groups(sizes, rows)
    count = count_of(sizes, scattered)
    chunk = rows // count
    sems = lambda n: [pltpu.SemaphoreType.DMA((max(n - 1, 1),))] * 2
    shapes = [[pltpu.VMEM((count, chunk, width), jnp.float32)] + sems(count)]
    for axis in whole:
        n = sizes[axis]
        shapes.append([pltpu.VMEM((n, chunk, width), jnp.float32)] + sems(n))
    shapes.append(sems(count))
    return shapes


def merged(sizes):
    found = {}
    for step in X_STEPS + Y_STEPS + XY_STEPS:
        found.setdefault(tuple(d % sizes[a] for a, d in zip(AXES, step)), []).append(step)
    return list(found.values())


def part_rows(step, count):
    return count * TILE * (SIDE if 0 in step[:2] else 1)


class Halo:
    def __init__(self, sizes, cells, work, z_send, z_recv, f_send, f_recv, sems):
        self.sizes, self.cells, self.work = sizes, cells, work
        self.z_send, self.z_recv = z_send, z_recv
        self.f_send, self.f_recv = f_send, f_recv
        self.send_sem, self.recv_sem = sems
        self.messages = merged(sizes)
        steps = Z_STEPS + tuple(steps[0] for steps in self.messages)
        self.places = {step: neighbour(sizes, step) for step in steps}

    def remote(self, slot, number, step, source, target):
        return pltpu.make_async_remote_copy(
            src_ref=source,
            dst_ref=target,
            send_sem=self.send_sem.at[slot, number],
            recv_sem=self.recv_sem.at[slot, number],
            device_id=self.places[step],
            device_id_type=MESH,
        )

    def lines(self, cell, step):
        first = cell * CELL_ROWS
        if step[1] == 0:
            return [pl.ds(first + side_of(step[0]) * SIDE * TILE, SIDE * TILE)]
        if step[0] == 0:
            rows = range(SIDE)
        else:
            rows = [side_of(step[0])]
        return [pl.ds(first + (a * SIDE + side_of(step[1])) * TILE, TILE) for a in rows]

    def send_faces(self, slot, group, cells):
        copies = []
        row = 0
        for n, steps in enumerate(self.messages):
            begin = row
            for step in steps:
                part = [self.work[at, :] for k in cells for at in self.lines(k, step)]
                size = part_rows(step, len(cells))
                self.f_send[slot, group, row : row + size, :] = jnp.concatenate(part, 0).astype(
                    self.f_send.dtype
                )
                row += size
            rows = pl.ds(begin, row - begin)
            copies.append(
                self.remote(
                    slot,
                    len(Z_STEPS) + group * len(self.messages) + n,
                    steps[0],
                    self.f_send.at[slot, group, rows],
                    self.f_recv.at[slot, group, rows],
                )
            )
            copies[-1].start()
        return copies

    def add_faces(self, slot, group, cells, copies):
        row = 0
        for copy, steps in zip(copies, self.messages):
            copy.wait()
            for step in steps:
                size = part_rows(step, len(cells))
                got = self.f_recv[slot, group, row : row + size, :].astype(jnp.float32)
                row += size
                taken = 0
                for k in cells:
                    for at in self.lines(k, tuple(-d for d in step)):
                        self.work[at, :] = self.work[at, :] + got[taken : taken + at.size]
                        taken += at.size

    def z_rows(self, cell, c):
        return pl.ds(cell * CELL_ROWS + c, LINES, stride=TILE)

    def z_copies(self, slot):
        return [
            self.remote(slot, n, step, self.z_send.at[slot, n], self.z_recv.at[slot, n])
            for n, step in enumerate(Z_STEPS)
        ]

    def send_z(self, slot):
        work = self.work
        self.z_send[slot, 0] = work[self.z_rows(self.cells - 1, ORDER), :]
        self.z_send[slot, 1] = work[self.z_rows(0, 0), :]
        for copy in self.z_copies(slot):
            copy.start()
        for cell in range(self.cells - 1):
            lower, upper = self.z_rows(cell, ORDER), self.z_rows(cell + 1, 0)
            both = work[lower, :] + work[upper, :]
            work[lower, :] = both
            work[upper, :] = both

    def add_z(self, slot):
        work = self.work
        for copy in self.z_copies(slot):
            copy.wait()
        bottom, top = self.z_rows(0, 0), self.z_rows(self.cells - 1, ORDER)
        work[bottom, :] = work[bottom, :] + self.z_recv[slot, 0]
        work[top, :] = work[top, :] + self.z_recv[slot, 1]


def inverse_factor(gram, mixed, inverse):
    n = gram.shape[0]
    size = BLOCK_ROWS if n % BLOCK_ROWS == 0 else TILE
    mixed[...] = gram
    sub = lax.broadcasted_iota(jnp.int32, (size, n), 0)
    col = lax.broadcasted_iota(jnp.int32, (size, n), 1)
    for start in range(0, n, size):
        end = start + size
        rows = mixed[start:end, :]
        cols = [jnp.broadcast_to(rows[:, start + t : start + t + 1], (size, n)) for t in range(size)]
        unit = jnp.where(col - start == sub, 1.0, 0.0).astype(jnp.float32)
        rows = jnp.where((col >= start) & (col < end), unit, rows)
        scale = jnp.zeros((size, n), jnp.float32)
        for s in range(size):
            root = lax.rsqrt(cols[s][s : s + 1, :])
            scale = jnp.where(sub == s, root, scale)
            if s + 1 < size:
                ratio = jnp.where(sub > s, cols[s] * (root * root), 0.0)
                for t in range(s + 1, size):
                    cols[t] = cols[t] - ratio * cols[t][s : s + 1, :]
                rows = rows - ratio * rows[s : s + 1, :]
        rows = rows * scale
        inverse[start:end, :] = jnp.where(col < end, rows, 0.0)
        if end < n:
            change = dot_rows(jnp.where(col >= end, rows, 0.0), rows, HIGHEST)[end:, :]
            rest = lax.broadcasted_iota(jnp.int32, (n - end, n), 1)
            kept = jnp.where((rest >= start) & (rest < end), 0.0, mixed[end:, :])
            mixed[end:, :] = kept - change


def kernel(
    sizes,
    cells,
    nodes_total,
    coef_ref,
    start_ref,
    locked_ref,
    h_ref,
    out_ref,
    padded_h,
    grid_nodes,
    state,
    work,
    z_send,
    z_recv,
    f_send,
    f_recv,
    halo_sems,
    locked_t,
    cross_part,
    cross_scratch,
    coefficient,
    gram_part,
    gram_scratch,
    gram_rows,
    parts,
    mixed,
    inverse,
):
    width = work.shape[1]
    node = h_ref.shape[1]
    steps = greeted(sizes, [groups(sizes, locked_ref.shape[1])[0], groups(sizes, width)[0], *[(a,) for a in AXES]])
    barrier = pltpu.get_barrier_semaphore()
    for step in steps:
        pl.semaphore_signal(
            barrier, inc=1, device_id=neighbour(sizes, step), device_id_type=MESH
        )

    own = start_ref.shape[2]
    grid_nodes[...] = jnp.zeros_like(grid_nodes)
    grid_nodes[:, :, :own, :] = start_ref[...].astype(jnp.float32)
    work[...] = jnp.zeros_like(work)
    sub = lax.broadcasted_iota(jnp.int32, (ORDER, TILE, width), 1)
    for k in range(cells):
        for a in range(ORDER):
            values = grid_nodes[a, :, ORDER * k : ORDER * k + TILE, :]
            first = k * CELL_ROWS + a * SIDE * TILE
            work[first : first + ORDER * TILE, :] = jnp.where(sub < ORDER, values, 0.0).reshape(
                ORDER * TILE, width
            )
    pl.semaphore_wait(barrier, len(steps))
    halo = Halo(sizes, cells, work, z_send, z_recv, f_send, f_recv, halo_sems)
    inner, outer = tuple(range(1, cells - 1)), (0, cells - 1)
    state[...] = jnp.zeros(state.shape, jnp.float32)

    def finish_faces(slot, inner_copies, outer_copies):
        halo.add_faces(slot, 0, inner, inner_copies)
        halo.add_faces(slot, 1, outer, outer_copies)
        halo.send_z(slot)

    def update(t, group):
        now, old = lax.rem(t, 2), lax.rem(t + 1, 2)
        scale, shift, back = coef_ref[t, 0], coef_ref[t, 1], coef_ref[t, 2]
        for k in group:
            rows = pl.ds(k * CELL_ROWS, CELL_ROWS)
            state[now, rows, :] = (
                scale * (work[rows, :] - shift * state[old, rows, :]) - back * state[now, rows, :]
            )

    def multiply(t, group):
        for k in group:
            rows = pl.ds(k * CELL_ROWS, CELL_ROWS)
            values = state[lax.rem(t, 2), rows, :].astype(jnp.bfloat16)
            work[rows, :] = jnp.dot(padded_h[k], values, preferred_element_type=jnp.float32)

    inner_copies = halo.send_faces(0, 0, inner)
    outer_copies = halo.send_faces(0, 1, outer)
    row = lax.broadcasted_iota(jnp.int32, (CELL_ROWS, node), 0)
    col = lax.broadcasted_iota(jnp.int32, (CELL_ROWS, node), 1)
    place = jnp.where(row % TILE < SIDE, row // TILE * SIDE + row % TILE, -1)
    spread = jnp.where(col == place, 1.0, 0.0).astype(jnp.bfloat16)
    for k in range(cells):
        tall = jnp.dot(spread, h_ref[k], preferred_element_type=jnp.float32).astype(jnp.bfloat16)
        padded_h[k] = lax.dot_general(
            tall, spread, (((1,), (1,)), ((), ())), preferred_element_type=jnp.float32
        ).astype(jnp.bfloat16)
    locked_t[...] = locked_ref[...].T
    finish_faces(0, inner_copies, outer_copies)

    def apply(t, carry):
        slot = lax.rem(t, 2)
        update(t - 1, inner)
        multiply(t - 1, inner)
        inner_copies = halo.send_faces(slot, 0, inner)
        halo.add_z(lax.rem(t - 1, 2))
        update(t - 1, outer)
        multiply(t - 1, outer)
        outer_copies = halo.send_faces(slot, 1, outer)
        finish_faces(slot, inner_copies, outer_copies)
        return carry

    lax.fori_loop(1, APPLY + 1, apply, 0)
    update(APPLY, inner)
    halo.add_z(APPLY % 2)
    update(APPLY, outer)
    last = APPLY % 2
    for k in range(cells):
        for a in range(ORDER):
            first = k * CELL_ROWS + a * SIDE * TILE
            grid_nodes[a, :, ORDER * k : ORDER * k + TILE, :] = state[
                last, first : first + ORDER * TILE, :
            ].reshape(ORDER, TILE, width)
    filtered = (
        grid_nodes[:, :, :own, :].reshape(ORDER * ORDER * own, width).astype(jnp.bfloat16)
    )
    cross_part[...] = jnp.dot(locked_t[...], filtered, preferred_element_type=jnp.float32)
    sum_over_devices(
        sizes,
        cross_part,
        cross_scratch,
        lambda total: (total / nodes_total).astype(jnp.bfloat16),
        coefficient,
    )
    projected = filtered.astype(jnp.float32) - jnp.dot(
        locked_ref[...],
        coefficient[...].reshape(locked_ref.shape[1], width),
        preferred_element_type=jnp.float32,
    )
    high, low = split(projected)
    parts[:, :width] = high
    parts[:, width:] = low
    terms = dot_rows(parts[...], parts[...])
    gram_part[...] = (
        terms[:width, :width]
        + (terms[:width, width:] + terms[width:, :width])
        + terms[width:, width:]
    )
    sum_over_devices(sizes, gram_part, gram_scratch, lambda total: total / nodes_total, gram_rows)
    inverse_factor(gram_rows[...].reshape(width, width), mixed, inverse)
    inverse_high, inverse_low = split(inverse[...])
    wide = jnp.concatenate([inverse_high, inverse_high], axis=1)
    contract = (((1,), (1,)), ((), ()))
    out_ref[...] = lax.dot_general(
        parts[...], wide, contract, preferred_element_type=jnp.float32
    ) + lax.dot_general(
        parts[:, :width], inverse_low, contract, preferred_element_type=jnp.float32
    )


def per_device(sizes, start_block, locked_orbitals, cell_h):
    width = start_block.shape[3]
    locked = locked_orbitals.shape[3]
    own = start_block.shape[2]
    cells = cell_h.shape[2]
    assert cell_h.shape[:2] == (1, 1)
    nodes = ORDER * ORDER * own
    nodes_total = float(nodes * count_of(sizes, AXES))
    count = lambda rows: count_of(sizes, groups(sizes, rows)[0])
    largest = max(cells - 2, 2)
    faces = sum(part_rows(step, largest) for step in X_STEPS + Y_STEPS + XY_STEPS)
    messages = len(Z_STEPS) + 2 * len(merged(sizes))
    vmem = pltpu.VMEM
    scratch = [
        vmem((cells, CELL_ROWS, CELL_ROWS), jnp.bfloat16),
        vmem((ORDER, ORDER, own + TILE, width), jnp.float32),
        vmem((2, cells * CELL_ROWS, width), jnp.float32),
        vmem((cells * CELL_ROWS, width), jnp.float32),
        vmem((2, 2, LINES, width), jnp.float32),
        vmem((2, 2, LINES, width), jnp.float32),
        vmem((2, 2, faces, width), jnp.bfloat16),
        vmem((2, 2, faces, width), jnp.bfloat16),
        [pltpu.SemaphoreType.DMA((2, messages))] * 2,
        vmem((locked, nodes), jnp.bfloat16),
        vmem((locked, width), jnp.float32),
        sum_scratch(sizes, locked, width),
        vmem((count(locked), locked // count(locked), width), jnp.bfloat16),
        vmem((width, width), jnp.float32),
        sum_scratch(sizes, width, width),
        vmem((count(width), width // count(width), width), jnp.float32),
        vmem((nodes, 2 * width), jnp.bfloat16),
        vmem((width, width), jnp.float32),
        vmem((width, width), jnp.float32),
    ]
    result = pl.pallas_call(
        functools.partial(kernel, sizes, cells, nodes_total),
        out_shape=jax.ShapeDtypeStruct((nodes, width), jnp.float32),
        in_specs=[pl.BlockSpec(memory_space=pltpu.SMEM)]
        + [pl.BlockSpec(memory_space=pltpu.VMEM)] * 3,
        out_specs=pl.BlockSpec(memory_space=pltpu.VMEM),
        scratch_shapes=scratch,
        compiler_params=pltpu.CompilerParams(
            collective_id=0, has_side_effects=True, vmem_limit_bytes=40 << 20
        ),
    )(
        jnp.asarray(recurrence()),
        start_block,
        locked_orbitals.reshape(nodes, locked),
        cell_h.reshape(cell_h.shape[2:]),
    )
    return result.reshape(start_block.shape)


def solution(mesh):
    sizes = dict(mesh.shape)
    placed = (P("gx", "gy", "gz", None), P("gx", "gy", "gz", None), P("gx", "gy", "gz", None, None))
    return jax.shard_map(
        functools.partial(per_device, sizes),
        mesh=mesh,
        in_specs=placed,
        out_specs=P("gx", "gy", "gz", None),
        check_vma=False,
    )
```

```python
import functools

import jax
import jax.numpy as jnp
import numpy as np
from jax import lax
from jax.experimental import pallas as pl
from jax.experimental.pallas import tpu as pltpu
from jax.sharding import PartitionSpec as P

ORDER = 6
SIDE = ORDER + 1
TILE = 8
LINES = SIDE * SIDE
CELL_ROWS = LINES * TILE
APPLY = 6
BLOCK_ROWS = 16
AXES = ("gx", "gy", "gz")

filter_low = 3.0
filter_high = 40.0
filter_bottom = 0.5

MESH = pl.DeviceIdType.MESH
HIGHEST = lax.Precision.HIGHEST

Z_STEPS = ((0, 0, 1), (0, 0, -1))
X_STEPS = ((1, 0, 0), (-1, 0, 0))
Y_STEPS = ((0, 1, 0), (0, -1, 0))
XY_STEPS = ((1, 1, 0), (1, -1, 0), (-1, 1, 0), (-1, -1, 0))


def recurrence():
    half = (filter_high - filter_low) / 2.0
    center = (filter_high + filter_low) / 2.0
    first = half / (filter_bottom - center)
    rows = [(1.0, 0.0, 0.0), (first / half, center, 0.0)]
    now = first
    for _ in range(APPLY - 1):
        later = 1.0 / (2.0 / first - now)
        rows.append((2.0 * later / half, center, now * later))
        now = later
    return np.asarray(rows, np.float32)


def side_of(step):
    return ORDER if step > 0 else 0


def dot_rows(a, b, precision=None):
    return lax.dot_general(
        a, b, (((0,), (0,)), ((), ())), precision=precision, preferred_element_type=jnp.float32
    )


def split(values):
    high = values.astype(jnp.bfloat16)
    return high, (values - high.astype(jnp.float32)).astype(jnp.bfloat16)


def groups(sizes, rows):
    for scattered in (("gy", "gz"), ("gz",)):
        count = int(np.prod([sizes[a] for a in scattered]))
        if rows % (16 * count) == 0:
            return scattered, tuple(a for a in AXES if a not in scattered)
    return (), AXES


def count_of(sizes, axes):
    return int(np.prod([sizes[a] for a in axes], dtype=np.int64))


def index_in(sizes, axes):
    index = 0
    for axis in axes:
        index = index * sizes[axis] + lax.axis_index(axis)
    return index


def device_at(sizes, axes, index):
    place = {axis: lax.axis_index(axis) for axis in AXES}
    for axis in reversed(axes):
        place[axis] = lax.rem(index, sizes[axis])
        index = index // sizes[axis]
    return tuple(place[axis] for axis in AXES)


def neighbour(sizes, step):
    return tuple(
        lax.rem(lax.axis_index(axis) + d + sizes[axis], sizes[axis]) for axis, d in zip(AXES, step)
    )


def greeted(sizes, all_axes):
    steps = {
        tuple(d % sizes[a] for a, d in zip(AXES, step))
        for step in Z_STEPS + X_STEPS + Y_STEPS + XY_STEPS
    }
    for axes in all_axes:
        for place in np.ndindex(*[sizes[a] for a in axes]):
            near = dict(zip(axes, place))
            steps.add(tuple(int(near.get(a, 0)) for a in AXES))
    steps.discard((0, 0, 0))
    return sorted(steps)


def exchange(sizes, axes, source, slots, send_sem, recv_sem):
    count = count_of(sizes, axes)
    me = index_in(sizes, axes)
    copies = []
    for r in range(1, count):
        place = lax.rem(me + r, count)
        copies.append(
            pltpu.make_async_remote_copy(
                src_ref=source(place),
                dst_ref=slots.at[me],
                send_sem=send_sem.at[r - 1],
                recv_sem=recv_sem.at[r - 1],
                device_id=device_at(sizes, axes, place),
                device_id_type=MESH,
            )
        )
    for copy in copies:
        copy.start()
    for copy in copies:
        copy.wait()


def sum_over_devices(sizes, part, scratch, finish, gathered):
    scattered, whole = groups(sizes, part.shape[0])
    if scattered:
        slots, send_sem, recv_sem = scratch[0]
        chunk = slots.shape[1]
        me = index_in(sizes, scattered)
        rows = lambda place: part.at[pl.ds(pl.multiple_of(place * chunk, chunk), chunk)]
        slots[me] = rows(me)[...]
        exchange(sizes, scattered, rows, slots, send_sem, recv_sem)
        total = jnp.sum(slots[...], axis=0)
    else:
        me = 0
        total = part[...]
    for axis, (slots, send_sem, recv_sem) in zip(whole, scratch[1:-1]):
        place = lax.axis_index(axis)
        slots[place] = total
        exchange(sizes, (axis,), lambda _: slots.at[place], slots, send_sem, recv_sem)
        total = jnp.sum(slots[...], axis=0)
    gathered[me] = finish(total)
    if scattered:
        send_sem, recv_sem = scratch[-1]
        exchange(sizes, scattered, lambda _: gathered.at[me], gathered, send_sem, recv_sem)


def sum_scratch(sizes, rows, width):
    scattered, whole = groups(sizes, rows)
    count = count_of(sizes, scattered)
    chunk = rows // count
    sems = lambda n: [pltpu.SemaphoreType.DMA((max(n - 1, 1),))] * 2
    shapes = [[pltpu.VMEM((count, chunk, width), jnp.float32)] + sems(count)]
    for axis in whole:
        n = sizes[axis]
        shapes.append([pltpu.VMEM((n, chunk, width), jnp.float32)] + sems(n))
    shapes.append(sems(count))
    return shapes


def merged(sizes):
    found = {}
    for step in X_STEPS + Y_STEPS + XY_STEPS:
        found.setdefault(tuple(d % sizes[a] for a, d in zip(AXES, step)), []).append(step)
    return list(found.values())


def part_rows(step, count):
    return count * TILE * (SIDE if 0 in step[:2] else 1)


class Halo:
    def __init__(self, sizes, cells, work, z_send, z_recv, f_send, f_recv, sems):
        self.sizes, self.cells, self.work = sizes, cells, work
        self.z_send, self.z_recv = z_send, z_recv
        self.f_send, self.f_recv = f_send, f_recv
        self.send_sem, self.recv_sem = sems
        self.messages = merged(sizes)
        steps = Z_STEPS + tuple(steps[0] for steps in self.messages)
        self.places = {step: neighbour(sizes, step) for step in steps}

    def remote(self, slot, number, step, source, target):
        return pltpu.make_async_remote_copy(
            src_ref=source,
            dst_ref=target,
            send_sem=self.send_sem.at[slot, number],
            recv_sem=self.recv_sem.at[slot, number],
            device_id=self.places[step],
            device_id_type=MESH,
        )

    def lines(self, cell, step):
        first = cell * CELL_ROWS
        if step[1] == 0:
            return [pl.ds(first + side_of(step[0]) * SIDE * TILE, SIDE * TILE)]
        if step[0] == 0:
            rows = range(SIDE)
        else:
            rows = [side_of(step[0])]
        return [pl.ds(first + (a * SIDE + side_of(step[1])) * TILE, TILE) for a in rows]

    def send_faces(self, slot, group, cells):
        copies = []
        row = 0
        for n, steps in enumerate(self.messages):
            begin = row
            for step in steps:
                part = [self.work[at, :] for k in cells for at in self.lines(k, step)]
                size = part_rows(step, len(cells))
                self.f_send[slot, group, row : row + size, :] = jnp.concatenate(part, 0).astype(
                    self.f_send.dtype
                )
                row += size
            rows = pl.ds(begin, row - begin)
            copies.append(
                self.remote(
                    slot,
                    len(Z_STEPS) + group * len(self.messages) + n,
                    steps[0],
                    self.f_send.at[slot, group, rows],
                    self.f_recv.at[slot, group, rows],
                )
            )
            copies[-1].start()
        return copies

    def add_faces(self, slot, group, cells, copies):
        row = 0
        for copy, steps in zip(copies, self.messages):
            copy.wait()
            for step in steps:
                size = part_rows(step, len(cells))
                got = self.f_recv[slot, group, row : row + size, :].astype(jnp.float32)
                row += size
                taken = 0
                for k in cells:
                    for at in self.lines(k, tuple(-d for d in step)):
                        self.work[at, :] = self.work[at, :] + got[taken : taken + at.size]
                        taken += at.size

    def z_rows(self, cell, c):
        return pl.ds(cell * CELL_ROWS + c, LINES, stride=TILE)

    def z_copies(self, slot):
        return [
            self.remote(slot, n, step, self.z_send.at[slot, n], self.z_recv.at[slot, n])
            for n, step in enumerate(Z_STEPS)
        ]

    def send_z(self, slot):
        work = self.work
        self.z_send[slot, 0] = work[self.z_rows(self.cells - 1, ORDER), :]
        self.z_send[slot, 1] = work[self.z_rows(0, 0), :]
        for copy in self.z_copies(slot):
            copy.start()
        for cell in range(self.cells - 1):
            lower, upper = self.z_rows(cell, ORDER), self.z_rows(cell + 1, 0)
            both = work[lower, :] + work[upper, :]
            work[lower, :] = both
            work[upper, :] = both

    def add_z(self, slot):
        work = self.work
        for copy in self.z_copies(slot):
            copy.wait()
        bottom, top = self.z_rows(0, 0), self.z_rows(self.cells - 1, ORDER)
        work[bottom, :] = work[bottom, :] + self.z_recv[slot, 0]
        work[top, :] = work[top, :] + self.z_recv[slot, 1]


def inverse_factor(gram, mixed, inverse):
    n = gram.shape[0]
    size = BLOCK_ROWS if n % BLOCK_ROWS == 0 else TILE
    mixed[...] = gram
    sub = lax.broadcasted_iota(jnp.int32, (size, n), 0)
    col = lax.broadcasted_iota(jnp.int32, (size, n), 1)
    for start in range(0, n, size):
        end = start + size
        rows = mixed[start:end, :]
        cols = [jnp.broadcast_to(rows[:, start + t : start + t + 1], (size, n)) for t in range(size)]
        unit = jnp.where(col - start == sub, 1.0, 0.0).astype(jnp.float32)
        rows = jnp.where((col >= start) & (col < end), unit, rows)
        scale = jnp.zeros((size, n), jnp.float32)
        for s in range(size):
            root = lax.rsqrt(cols[s][s : s + 1, :])
            scale = jnp.where(sub == s, root, scale)
            if s + 1 < size:
                ratio = jnp.where(sub > s, cols[s] * (root * root), 0.0)
                for t in range(s + 1, size):
                    cols[t] = cols[t] - ratio * cols[t][s : s + 1, :]
                rows = rows - ratio * rows[s : s + 1, :]
        rows = rows * scale
        inverse[start:end, :] = jnp.where(col < end, rows, 0.0)
        if end < n:
            change = dot_rows(jnp.where(col >= end, rows, 0.0), rows, HIGHEST)[end:, :]
            rest = lax.broadcasted_iota(jnp.int32, (n - end, n), 1)
            kept = jnp.where((rest >= start) & (rest < end), 0.0, mixed[end:, :])
            mixed[end:, :] = kept - change


def kernel(
    sizes,
    cells,
    nodes_total,
    coef_ref,
    start_ref,
    locked_ref,
    h_ref,
    parts,
    gram_rows,
    padded_h,
    grid_nodes,
    state,
    work,
    z_send,
    z_recv,
    f_send,
    f_recv,
    halo_sems,
    locked_t,
    cross_part,
    cross_scratch,
    coefficient,
    gram_part,
    gram_scratch,
):
    width = work.shape[1]
    node = h_ref.shape[1]
    steps = greeted(sizes, [groups(sizes, locked_ref.shape[1])[0], groups(sizes, width)[0], *[(a,) for a in AXES]])
    barrier = pltpu.get_barrier_semaphore()
    for step in steps:
        pl.semaphore_signal(
            barrier, inc=1, device_id=neighbour(sizes, step), device_id_type=MESH
        )

    own = start_ref.shape[2]
    grid_nodes[...] = jnp.zeros_like(grid_nodes)
    grid_nodes[:, :, :own, :] = start_ref[...].astype(jnp.float32)
    work[...] = jnp.zeros_like(work)
    sub = lax.broadcasted_iota(jnp.int32, (ORDER, TILE, width), 1)
    for k in range(cells):
        for a in range(ORDER):
            values = grid_nodes[a, :, ORDER * k : ORDER * k + TILE, :]
            first = k * CELL_ROWS + a * SIDE * TILE
            work[first : first + ORDER * TILE, :] = jnp.where(sub < ORDER, values, 0.0).reshape(
                ORDER * TILE, width
            )
    pl.semaphore_wait(barrier, len(steps))
    halo = Halo(sizes, cells, work, z_send, z_recv, f_send, f_recv, halo_sems)
    inner, outer = tuple(range(1, cells - 1)), (0, cells - 1)
    state[...] = jnp.zeros(state.shape, jnp.float32)

    def finish_faces(slot, inner_copies, outer_copies):
        halo.add_faces(slot, 0, inner, inner_copies)
        halo.add_faces(slot, 1, outer, outer_copies)
        halo.send_z(slot)

    def update(t, group):
        now, old = lax.rem(t, 2), lax.rem(t + 1, 2)
        scale, shift, back = coef_ref[t, 0], coef_ref[t, 1], coef_ref[t, 2]
        for k in group:
            rows = pl.ds(k * CELL_ROWS, CELL_ROWS)
            state[now, rows, :] = (
                scale * (work[rows, :] - shift * state[old, rows, :]) - back * state[now, rows, :]
            )

    def multiply(t, group):
        for k in group:
            rows = pl.ds(k * CELL_ROWS, CELL_ROWS)
            values = state[lax.rem(t, 2), rows, :].astype(jnp.bfloat16)
            work[rows, :] = jnp.dot(padded_h[k], values, preferred_element_type=jnp.float32)

    inner_copies = halo.send_faces(0, 0, inner)
    outer_copies = halo.send_faces(0, 1, outer)
    row = lax.broadcasted_iota(jnp.int32, (CELL_ROWS, node), 0)
    col = lax.broadcasted_iota(jnp.int32, (CELL_ROWS, node), 1)
    place = jnp.where(row % TILE < SIDE, row // TILE * SIDE + row % TILE, -1)
    spread = jnp.where(col == place, 1.0, 0.0).astype(jnp.bfloat16)
    for k in range(cells):
        tall = jnp.dot(spread, h_ref[k], preferred_element_type=jnp.float32).astype(jnp.bfloat16)
        padded_h[k] = lax.dot_general(
            tall, spread, (((1,), (1,)), ((), ())), preferred_element_type=jnp.float32
        ).astype(jnp.bfloat16)
    locked_t[...] = locked_ref[...].T
    finish_faces(0, inner_copies, outer_copies)

    def apply(t, carry):
        slot = lax.rem(t, 2)
        update(t - 1, inner)
        multiply(t - 1, inner)
        inner_copies = halo.send_faces(slot, 0, inner)
        halo.add_z(lax.rem(t - 1, 2))
        update(t - 1, outer)
        multiply(t - 1, outer)
        outer_copies = halo.send_faces(slot, 1, outer)
        finish_faces(slot, inner_copies, outer_copies)
        return carry

    lax.fori_loop(1, APPLY + 1, apply, 0)
    update(APPLY, inner)
    halo.add_z(APPLY % 2)
    update(APPLY, outer)
    last = APPLY % 2
    for k in range(cells):
        for a in range(ORDER):
            first = k * CELL_ROWS + a * SIDE * TILE
            grid_nodes[a, :, ORDER * k : ORDER * k + TILE, :] = state[
                last, first : first + ORDER * TILE, :
            ].reshape(ORDER, TILE, width)
    filtered = (
        grid_nodes[:, :, :own, :].reshape(ORDER * ORDER * own, width).astype(jnp.bfloat16)
    )
    cross_part[...] = jnp.dot(locked_t[...], filtered, preferred_element_type=jnp.float32)
    sum_over_devices(
        sizes,
        cross_part,
        cross_scratch,
        lambda total: (total / nodes_total).astype(jnp.bfloat16),
        coefficient,
    )
    projected = filtered.astype(jnp.float32) - jnp.dot(
        locked_ref[...],
        coefficient[...].reshape(locked_ref.shape[1], width),
        preferred_element_type=jnp.float32,
    )
    high, low = split(projected)
    parts[:, :width] = high
    parts[:, width:] = low
    terms = dot_rows(parts[...], parts[...])
    gram_part[...] = (
        terms[:width, :width]
        + (terms[:width, width:] + terms[width:, :width])
        + terms[width:, width:]
    )
    sum_over_devices(sizes, gram_part, gram_scratch, lambda total: total / nodes_total, gram_rows)


def finish_kernel(parts, gram_rows, out_ref, mixed, inverse):
    width = out_ref.shape[1]
    inverse_factor(gram_rows[...].reshape(width, width), mixed, inverse)
    inverse_high, inverse_low = split(inverse[...])
    wide = jnp.concatenate([inverse_high, inverse_high], axis=1)
    contract = (((1,), (1,)), ((), ()))
    out_ref[...] = lax.dot_general(
        parts[...], wide, contract, preferred_element_type=jnp.float32
    ) + lax.dot_general(
        parts[:, :width], inverse_low, contract, preferred_element_type=jnp.float32
    )


def per_device(sizes, start_block, locked_orbitals, cell_h):
    width = start_block.shape[3]
    locked = locked_orbitals.shape[3]
    own = start_block.shape[2]
    cells = cell_h.shape[2]
    assert cell_h.shape[:2] == (1, 1)
    nodes = ORDER * ORDER * own
    nodes_total = float(nodes * count_of(sizes, AXES))
    count = lambda rows: count_of(sizes, groups(sizes, rows)[0])
    largest = max(cells - 2, 2)
    faces = sum(part_rows(step, largest) for step in X_STEPS + Y_STEPS + XY_STEPS)
    messages = len(Z_STEPS) + 2 * len(merged(sizes))
    vmem = pltpu.VMEM
    scratch = [
        vmem((cells, CELL_ROWS, CELL_ROWS), jnp.bfloat16),
        vmem((ORDER, ORDER, own + TILE, width), jnp.float32),
        vmem((2, cells * CELL_ROWS, width), jnp.float32),
        vmem((cells * CELL_ROWS, width), jnp.float32),
        vmem((2, 2, LINES, width), jnp.float32),
        vmem((2, 2, LINES, width), jnp.float32),
        vmem((2, 2, faces, width), jnp.bfloat16),
        vmem((2, 2, faces, width), jnp.bfloat16),
        [pltpu.SemaphoreType.DMA((2, messages))] * 2,
        vmem((locked, nodes), jnp.bfloat16),
        vmem((locked, width), jnp.float32),
        sum_scratch(sizes, locked, width),
        vmem((count(locked), locked // count(locked), width), jnp.bfloat16),
        vmem((width, width), jnp.float32),
        sum_scratch(sizes, width, width),
    ]
    block = pl.BlockSpec(memory_space=pltpu.VMEM)
    parts, gram = pl.pallas_call(
        functools.partial(kernel, sizes, cells, nodes_total),
        out_shape=(
            jax.ShapeDtypeStruct((nodes, 2 * width), jnp.bfloat16),
            jax.ShapeDtypeStruct((count(width), width // count(width), width), jnp.float32),
        ),
        in_specs=[pl.BlockSpec(memory_space=pltpu.SMEM)]
        + [block] * 3,
        out_specs=(block, block),
        scratch_shapes=scratch,
        compiler_params=pltpu.CompilerParams(
            collective_id=0, has_side_effects=True, vmem_limit_bytes=40 << 20
        ),
    )(
        jnp.asarray(recurrence()),
        start_block,
        locked_orbitals.reshape(nodes, locked),
        cell_h.reshape(cell_h.shape[2:]),
    )
    result = pl.pallas_call(
        finish_kernel,
        out_shape=jax.ShapeDtypeStruct((nodes, width), jnp.float32),
        in_specs=[block, block],
        out_specs=block,
        scratch_shapes=[vmem((width, width), jnp.float32), vmem((width, width), jnp.float32)],
        compiler_params=pltpu.CompilerParams(vmem_limit_bytes=16 << 20),
    )(parts, gram)
    return result.reshape(start_block.shape)


def solution(mesh):
    sizes = dict(mesh.shape)
    placed = (P("gx", "gy", "gz", None), P("gx", "gy", "gz", None), P("gx", "gy", "gz", None, None))
    return jax.shard_map(
        functools.partial(per_device, sizes),
        mesh=mesh,
        in_specs=placed,
        out_specs=P("gx", "gy", "gz", None),
        check_vma=False,
    )
```

```python
import functools

import jax
import jax.numpy as jnp
import numpy as np
from jax import lax
from jax.experimental import pallas as pl
from jax.experimental.pallas import tpu as pltpu
from jax.sharding import PartitionSpec as P

ORDER = 6
SIDE = ORDER + 1
TILE = 8
LINES = SIDE * SIDE
CELL_ROWS = LINES * TILE
APPLY = 6
BLOCK_ROWS = 16
AXES = ("gx", "gy", "gz")

filter_low = 3.0
filter_high = 40.0
filter_bottom = 0.5

MESH = pl.DeviceIdType.MESH
HIGHEST = lax.Precision.HIGHEST

Z_STEPS = ((0, 0, 1), (0, 0, -1))
X_STEPS = ((1, 0, 0), (-1, 0, 0))
Y_STEPS = ((0, 1, 0), (0, -1, 0))
XY_STEPS = ((1, 1, 0), (1, -1, 0), (-1, 1, 0), (-1, -1, 0))


def recurrence():
    half = (filter_high - filter_low) / 2.0
    center = (filter_high + filter_low) / 2.0
    first = half / (filter_bottom - center)
    rows = [(1.0, 0.0, 0.0), (first / half, center, 0.0)]
    now = first
    for _ in range(APPLY - 1):
        later = 1.0 / (2.0 / first - now)
        rows.append((2.0 * later / half, center, now * later))
        now = later
    return np.asarray(rows, np.float32)


def side_of(step):
    return ORDER if step > 0 else 0


def dot_rows(a, b, precision=None):
    return lax.dot_general(
        a, b, (((0,), (0,)), ((), ())), precision=precision, preferred_element_type=jnp.float32
    )


def split(values):
    high = values.astype(jnp.bfloat16)
    return high, (values - high.astype(jnp.float32)).astype(jnp.bfloat16)


def groups(sizes, rows):
    for scattered in (("gy", "gz"), ("gz",)):
        count = int(np.prod([sizes[a] for a in scattered]))
        if rows % (16 * count) == 0:
            return scattered, tuple(a for a in AXES if a not in scattered)
    return (), AXES


def count_of(sizes, axes):
    return int(np.prod([sizes[a] for a in axes], dtype=np.int64))


def index_in(sizes, axes):
    index = 0
    for axis in axes:
        index = index * sizes[axis] + lax.axis_index(axis)
    return index


def device_at(sizes, axes, index):
    place = {axis: lax.axis_index(axis) for axis in AXES}
    for axis in reversed(axes):
        place[axis] = lax.rem(index, sizes[axis])
        index = index // sizes[axis]
    return tuple(place[axis] for axis in AXES)


def neighbour(sizes, step):
    return tuple(
        lax.rem(lax.axis_index(axis) + d + sizes[axis], sizes[axis]) for axis, d in zip(AXES, step)
    )


def greeted(sizes, all_axes):
    steps = {
        tuple(d % sizes[a] for a, d in zip(AXES, step))
        for step in Z_STEPS + X_STEPS + Y_STEPS + XY_STEPS
    }
    for axes in all_axes:
        for place in np.ndindex(*[sizes[a] for a in axes]):
            near = dict(zip(axes, place))
            steps.add(tuple(int(near.get(a, 0)) for a in AXES))
    steps.discard((0, 0, 0))
    return sorted(steps)


def exchange(sizes, axes, source, slots, send_sem, recv_sem):
    count = count_of(sizes, axes)
    me = index_in(sizes, axes)
    copies = []
    for r in range(1, count):
        place = lax.rem(me + r, count)
        copies.append(
            pltpu.make_async_remote_copy(
                src_ref=source(place),
                dst_ref=slots.at[me],
                send_sem=send_sem.at[r - 1],
                recv_sem=recv_sem.at[r - 1],
                device_id=device_at(sizes, axes, place),
                device_id_type=MESH,
            )
        )
    for copy in copies:
        copy.start()
    for copy in copies:
        copy.wait()


def sum_over_devices(sizes, part, scratch, finish, gathered):
    scattered, whole = groups(sizes, part.shape[0])
    if scattered:
        slots, send_sem, recv_sem = scratch[0]
        chunk = slots.shape[1]
        me = index_in(sizes, scattered)
        rows = lambda place: part.at[pl.ds(pl.multiple_of(place * chunk, chunk), chunk)]
        slots[me] = rows(me)[...]
        exchange(sizes, scattered, rows, slots, send_sem, recv_sem)
        total = jnp.sum(slots[...], axis=0)
    else:
        me = 0
        total = part[...]
    for axis, (slots, send_sem, recv_sem) in zip(whole, scratch[1:-1]):
        place = lax.axis_index(axis)
        slots[place] = total
        exchange(sizes, (axis,), lambda _: slots.at[place], slots, send_sem, recv_sem)
        total = jnp.sum(slots[...], axis=0)
    gathered[me] = finish(total)
    if scattered:
        send_sem, recv_sem = scratch[-1]
        exchange(sizes, scattered, lambda _: gathered.at[me], gathered, send_sem, recv_sem)


def sum_scratch(sizes, rows, width):
    scattered, whole = groups(sizes, rows)
    count = count_of(sizes, scattered)
    chunk = rows // count
    sems = lambda n: [pltpu.SemaphoreType.DMA((max(n - 1, 1),))] * 2
    shapes = [[pltpu.VMEM((count, chunk, width), jnp.float32)] + sems(count)]
    for axis in whole:
        n = sizes[axis]
        shapes.append([pltpu.VMEM((n, chunk, width), jnp.float32)] + sems(n))
    shapes.append(sems(count))
    return shapes


def merged(sizes):
    found = {}
    for step in X_STEPS + Y_STEPS + XY_STEPS:
        found.setdefault(tuple(d % sizes[a] for a, d in zip(AXES, step)), []).append(step)
    return list(found.values())


def part_rows(step, count):
    return count * TILE * (SIDE if 0 in step[:2] else 1)


class Halo:
    def __init__(self, sizes, half, pairs, work, z_send, z_recv, f_send, f_recv, sems, places):
        self.half, self.pairs, self.work = half, pairs, work
        self.z_send, self.z_recv = z_send, z_recv
        self.f_send, self.f_recv = f_send, f_recv
        self.send_sem, self.recv_sem = sems
        self.messages = merged(sizes)
        self.places = places
        self.side = work.shape[1] // 2
        self.low = lax.broadcasted_iota(jnp.int32, (LINES, work.shape[1]), 1) < self.side

    def remote(self, slot, number, step, source, target):
        return pltpu.make_async_remote_copy(
            src_ref=source,
            dst_ref=target,
            send_sem=self.send_sem.at[slot, number],
            recv_sem=self.recv_sem.at[slot, number],
            device_id=self.places[step],
            device_id_type=MESH,
        )

    def lines(self, cell, step):
        first = cell * CELL_ROWS
        if step[1] == 0:
            return [pl.ds(first + side_of(step[0]) * SIDE * TILE, SIDE * TILE)]
        if step[0] == 0:
            rows = range(SIDE)
        else:
            rows = [side_of(step[0])]
        return [pl.ds(first + (a * SIDE + side_of(step[1])) * TILE, TILE) for a in rows]

    def face_copies(self, slot):
        copies = []
        row = 0
        for n, steps in enumerate(self.messages):
            size = sum(part_rows(step, self.pairs) for step in steps)
            rows = pl.ds(row, size)
            row += size
            copies.append(
                self.remote(
                    slot,
                    2 * len(Z_STEPS) + self.half * len(self.messages) + n,
                    steps[0],
                    self.f_send.at[slot, self.half, rows],
                    self.f_recv.at[slot, self.half, rows],
                )
            )
        return copies

    def send_faces(self, slot):
        row = 0
        for copy, steps in zip(self.face_copies(slot), self.messages):
            for step in steps:
                part = [self.work[at, :] for k in range(self.pairs) for at in self.lines(k, step)]
                size = part_rows(step, self.pairs)
                self.f_send[slot, self.half, row : row + size, :] = jnp.concatenate(
                    part, 0
                ).astype(self.f_send.dtype)
                row += size
            copy.start()

    def add_faces(self, slot):
        row = 0
        for copy, steps in zip(self.face_copies(slot), self.messages):
            copy.wait()
            for step in steps:
                size = part_rows(step, self.pairs)
                got = self.f_recv[slot, self.half, row : row + size, :].astype(jnp.float32)
                row += size
                taken = 0
                for k in range(self.pairs):
                    for at in self.lines(k, tuple(-d for d in step)):
                        self.work[at, :] = self.work[at, :] + got[taken : taken + at.size]
                        taken += at.size

    def z_rows(self, pair, c):
        return pl.ds(pair * CELL_ROWS + c, LINES, stride=TILE)

    def z_copies(self, slot):
        first = self.half * len(Z_STEPS)
        return [
            self.remote(slot, n, step, self.z_send.at[slot, n], self.z_recv.at[slot, n])
            for n, step in enumerate(Z_STEPS, first)
        ]

    def send_z(self, slot):
        work = self.work
        first = self.half * len(Z_STEPS)
        bottom_rows, top_rows = self.z_rows(0, 0), self.z_rows(self.pairs - 1, ORDER)
        bottom, top = work[bottom_rows, :], pltpu.roll(work[top_rows, :], self.side, 1)
        self.z_send[slot, first] = top
        self.z_send[slot, first + 1] = bottom
        for copy in self.z_copies(slot):
            copy.start()
        for pair in range(self.pairs - 1):
            lower, upper = self.z_rows(pair, ORDER), self.z_rows(pair + 1, 0)
            both = work[lower, :] + work[upper, :]
            work[lower, :] = both
            work[upper, :] = both
        both = bottom + top
        work[bottom_rows, :] = jnp.where(self.low, bottom, both)
        work[top_rows, :] = pltpu.roll(jnp.where(self.low, top, both), self.side, 1)

    def add_z(self, slot):
        work = self.work
        first = self.half * len(Z_STEPS)
        for copy in self.z_copies(slot):
            copy.wait()
        bottom, top = self.z_rows(0, 0), self.z_rows(self.pairs - 1, ORDER)
        below = jnp.where(self.low, self.z_recv[slot, first], 0.0)
        above = jnp.where(self.low, self.z_recv[slot, first + 1], 0.0)
        work[bottom, :] = work[bottom, :] + below
        work[top, :] = work[top, :] + pltpu.roll(above, self.side, 1)


def inverse_factor(gram, mixed, inverse):
    n = gram.shape[0]
    size = BLOCK_ROWS if n % BLOCK_ROWS == 0 else TILE
    mixed[...] = gram
    sub = lax.broadcasted_iota(jnp.int32, (size, n), 0)
    col = lax.broadcasted_iota(jnp.int32, (size, n), 1)
    for start in range(0, n, size):
        end = start + size
        rows = mixed[start:end, :]
        cols = [jnp.broadcast_to(rows[:, start + t : start + t + 1], (size, n)) for t in range(size)]
        unit = jnp.where(col - start == sub, 1.0, 0.0).astype(jnp.float32)
        rows = jnp.where((col >= start) & (col < end), unit, rows)
        scale = jnp.zeros((size, n), jnp.float32)
        for s in range(size):
            root = lax.rsqrt(cols[s][s : s + 1, :])
            scale = jnp.where(sub == s, root, scale)
            if s + 1 < size:
                ratio = jnp.where(sub > s, cols[s] * (root * root), 0.0)
                for t in range(s + 1, size):
                    cols[t] = cols[t] - ratio * cols[t][s : s + 1, :]
                rows = rows - ratio * rows[s : s + 1, :]
        rows = rows * scale
        inverse[start:end, :] = jnp.where(col < end, rows, 0.0)
        if end < n:
            change = dot_rows(jnp.where(col >= end, rows, 0.0), rows, HIGHEST)[end:, :]
            rest = lax.broadcasted_iota(jnp.int32, (n - end, n), 1)
            kept = jnp.where((rest >= start) & (rest < end), 0.0, mixed[end:, :])
            mixed[end:, :] = kept - change


def kernel(
    sizes,
    cells,
    nodes_total,
    coef_ref,
    start_ref,
    locked_ref,
    h_ref,
    parts,
    gram_rows,
    padded_h,
    grid_nodes,
    state,
    work,
    z_send,
    z_recv,
    f_send,
    f_recv,
    halo_sems,
    locked_t,
    cross_part,
    cross_scratch,
    coefficient,
    gram_part,
    gram_scratch,
):
    width = work.shape[2]
    node = h_ref.shape[1]
    pairs = cells // 2
    steps = greeted(sizes, [groups(sizes, locked_ref.shape[1])[0], groups(sizes, width)[0], *[(a,) for a in AXES]])
    barrier = pltpu.get_barrier_semaphore()
    for step in steps:
        pl.semaphore_signal(
            barrier, inc=1, device_id=neighbour(sizes, step), device_id_type=MESH
        )

    own = start_ref.shape[2]
    grid_nodes[...] = jnp.zeros_like(grid_nodes)
    grid_nodes[:, :, :own, :] = start_ref[...].astype(jnp.float32)
    work[...] = jnp.zeros_like(work)
    tile_rows = ORDER * TILE
    side = width // 2
    low = lax.broadcasted_iota(jnp.int32, (tile_rows, width), 1) < side
    owned = lax.broadcasted_iota(jnp.int32, (tile_rows, width), 0) % TILE < ORDER
    for p in range(pairs):
        for a in range(ORDER):
            lower, upper = [
                grid_nodes[a, :, ORDER * k : ORDER * k + TILE, :].reshape(tile_rows, width)
                for k in (p, p + pairs)
            ]
            first = p * CELL_ROWS + a * SIDE * TILE
            one = jnp.where(low, lower, pltpu.roll(upper, side, 1))
            two = jnp.where(low, pltpu.roll(lower, side, 1), upper)
            work[0, first : first + tile_rows, :] = jnp.where(owned, one, 0.0)
            work[1, first : first + tile_rows, :] = jnp.where(owned, two, 0.0)
    pl.semaphore_wait(barrier, len(steps))
    places = {
        step: neighbour(sizes, step)
        for step in Z_STEPS + tuple(message[0] for message in merged(sizes))
    }
    halos = [
        Halo(
            sizes, h, pairs, work.at[h], z_send, z_recv, f_send, f_recv, halo_sems, places
        )
        for h in range(2)
    ]
    state[...] = jnp.zeros(state.shape, jnp.float32)
    low_lanes = lax.broadcasted_iota(jnp.int32, (CELL_ROWS, width), 1) < side

    def update(t, h):
        now, old = lax.rem(t, 2), lax.rem(t + 1, 2)
        scale, shift, back = coef_ref[t, 0], coef_ref[t, 1], coef_ref[t, 2]
        for p in range(pairs):
            rows = pl.ds(p * CELL_ROWS, CELL_ROWS)
            state[now, h, rows, :] = (
                scale * (work[h, rows, :] - shift * state[old, h, rows, :])
                - back * state[now, h, rows, :]
            )

    def multiply(t, h):
        for p in range(pairs):
            rows = pl.ds(p * CELL_ROWS, CELL_ROWS)
            values = state[lax.rem(t, 2), h, rows, :].astype(jnp.bfloat16)
            lower, upper = [
                jnp.dot(padded_h[k], values, preferred_element_type=jnp.float32)
                for k in (p, p + pairs)
            ]
            work[h, rows, :] = jnp.where(low_lanes, lower, upper)

    for halo in halos:
        halo.send_faces(0)
    row = lax.broadcasted_iota(jnp.int32, (CELL_ROWS, node), 0)
    col = lax.broadcasted_iota(jnp.int32, (CELL_ROWS, node), 1)
    place = jnp.where(row % TILE < SIDE, row // TILE * SIDE + row % TILE, -1)
    spread = jnp.where(col == place, 1.0, 0.0).astype(jnp.bfloat16)
    for k in range(cells):
        tall = jnp.dot(spread, h_ref[k], preferred_element_type=jnp.float32).astype(jnp.bfloat16)
        padded_h[k] = lax.dot_general(
            tall, spread, (((1,), (1,)), ((), ())), preferred_element_type=jnp.float32
        ).astype(jnp.bfloat16)
    locked_t[...] = locked_ref[...].T

    def apply(t, carry):
        slot, before = lax.rem(t, 2), lax.rem(t - 1, 2)
        for h, halo in enumerate(halos):
            halo.add_faces(before)
            halo.send_z(before)
            halo.add_z(before)
            update(t - 1, h)
            multiply(t - 1, h)
            halo.send_faces(slot)
        return carry

    lax.fori_loop(1, APPLY + 1, apply, 0)
    last = APPLY % 2
    for halo in halos:
        halo.add_faces(last)
        halo.send_z(last)
    for h, halo in enumerate(halos):
        halo.add_z(last)
        update(APPLY, h)
    for k in range(cells):
        p, upper = k % pairs, k >= pairs
        for a in range(ORDER):
            first = p * CELL_ROWS + a * SIDE * TILE
            one, two = [state[last, h, first : first + tile_rows, :] for h in range(2)]
            if upper:
                values = jnp.where(low, pltpu.roll(one, side, 1), two)
            else:
                values = jnp.where(low, one, pltpu.roll(two, side, 1))
            grid_nodes[a, :, ORDER * k : ORDER * k + TILE, :] = values.reshape(ORDER, TILE, width)
    filtered = (
        grid_nodes[:, :, :own, :].reshape(ORDER * ORDER * own, width).astype(jnp.bfloat16)
    )
    cross_part[...] = jnp.dot(locked_t[...], filtered, preferred_element_type=jnp.float32)
    sum_over_devices(
        sizes,
        cross_part,
        cross_scratch,
        lambda total: (total / nodes_total).astype(jnp.bfloat16),
        coefficient,
    )
    projected = filtered.astype(jnp.float32) - jnp.dot(
        locked_ref[...],
        coefficient[...].reshape(locked_ref.shape[1], width),
        preferred_element_type=jnp.float32,
    )
    high, low = split(projected)
    parts[:, :width] = high
    parts[:, width:] = low
    terms = dot_rows(parts[...], parts[...])
    gram_part[...] = (
        terms[:width, :width]
        + (terms[:width, width:] + terms[width:, :width])
        + terms[width:, width:]
    )
    sum_over_devices(sizes, gram_part, gram_scratch, lambda total: total / nodes_total, gram_rows)


def finish_kernel(parts, gram_rows, out_ref, mixed, inverse):
    width = out_ref.shape[1]
    inverse_factor(gram_rows[...].reshape(width, width), mixed, inverse)
    inverse_high, inverse_low = split(inverse[...])
    wide = jnp.concatenate([inverse_high, inverse_high], axis=1)
    contract = (((1,), (1,)), ((), ()))
    out_ref[...] = lax.dot_general(
        parts[...], wide, contract, preferred_element_type=jnp.float32
    ) + lax.dot_general(
        parts[:, :width], inverse_low, contract, preferred_element_type=jnp.float32
    )


def per_device(sizes, start_block, locked_orbitals, cell_h):
    width = start_block.shape[3]
    locked = locked_orbitals.shape[3]
    own = start_block.shape[2]
    cells = cell_h.shape[2]
    assert cell_h.shape[:2] == (1, 1)
    nodes = ORDER * ORDER * own
    nodes_total = float(nodes * count_of(sizes, AXES))
    count = lambda rows: count_of(sizes, groups(sizes, rows)[0])
    pairs = cells // 2
    assert cells == 2 * pairs
    faces = sum(part_rows(step, pairs) for step in X_STEPS + Y_STEPS + XY_STEPS)
    messages = 2 * (len(Z_STEPS) + len(merged(sizes)))
    vmem = pltpu.VMEM
    scratch = [
        vmem((cells, CELL_ROWS, CELL_ROWS), jnp.bfloat16),
        vmem((ORDER, ORDER, own + TILE, width), jnp.float32),
        vmem((2, 2, pairs * CELL_ROWS, width), jnp.float32),
        vmem((2, pairs * CELL_ROWS, width), jnp.float32),
        vmem((2, 4, LINES, width), jnp.float32),
        vmem((2, 4, LINES, width), jnp.float32),
        vmem((2, 2, faces, width), jnp.bfloat16),
        vmem((2, 2, faces, width), jnp.bfloat16),
        [pltpu.SemaphoreType.DMA((2, messages))] * 2,
        vmem((locked, nodes), jnp.bfloat16),
        vmem((locked, width), jnp.float32),
        sum_scratch(sizes, locked, width),
        vmem((count(locked), locked // count(locked), width), jnp.bfloat16),
        vmem((width, width), jnp.float32),
        sum_scratch(sizes, width, width),
    ]
    block = pl.BlockSpec(memory_space=pltpu.VMEM)
    parts, gram = pl.pallas_call(
        functools.partial(kernel, sizes, cells, nodes_total),
        out_shape=(
            jax.ShapeDtypeStruct((nodes, 2 * width), jnp.bfloat16),
            jax.ShapeDtypeStruct((count(width), width // count(width), width), jnp.float32),
        ),
        in_specs=[pl.BlockSpec(memory_space=pltpu.SMEM)]
        + [block] * 3,
        out_specs=(block, block),
        scratch_shapes=scratch,
        compiler_params=pltpu.CompilerParams(
            collective_id=0, has_side_effects=True, vmem_limit_bytes=40 << 20
        ),
    )(
        jnp.asarray(recurrence()),
        start_block,
        locked_orbitals.reshape(nodes, locked),
        cell_h.reshape(cell_h.shape[2:]),
    )
    result = pl.pallas_call(
        finish_kernel,
        out_shape=jax.ShapeDtypeStruct((nodes, width), jnp.float32),
        in_specs=[block, block],
        out_specs=block,
        scratch_shapes=[vmem((width, width), jnp.float32), vmem((width, width), jnp.float32)],
        compiler_params=pltpu.CompilerParams(vmem_limit_bytes=16 << 20),
    )(parts, gram)
    return result.reshape(start_block.shape)


def solution(mesh):
    sizes = dict(mesh.shape)
    placed = (P("gx", "gy", "gz", None), P("gx", "gy", "gz", None), P("gx", "gy", "gz", None, None))
    return jax.shard_map(
        functools.partial(per_device, sizes),
        mesh=mesh,
        in_specs=placed,
        out_specs=P("gx", "gy", "gz", None),
        check_vma=False,
    )
```

```python
import functools

import jax
import jax.numpy as jnp
import numpy as np
from jax import lax
from jax.experimental import pallas as pl
from jax.experimental.pallas import tpu as pltpu
from jax.sharding import PartitionSpec as P

ORDER = 6
SIDE = ORDER + 1
TILE = 8
LINES = SIDE * SIDE
CELL_ROWS = LINES * TILE
APPLY = 6
BLOCK_ROWS = 16
AXES = ("gx", "gy", "gz")

filter_low = 3.0
filter_high = 40.0
filter_bottom = 0.5

MESH = pl.DeviceIdType.MESH
HIGHEST = lax.Precision.HIGHEST

Z_STEPS = ((0, 0, 1), (0, 0, -1))
X_STEPS = ((1, 0, 0), (-1, 0, 0))
Y_STEPS = ((0, 1, 0), (0, -1, 0))
XY_STEPS = ((1, 1, 0), (1, -1, 0), (-1, 1, 0), (-1, -1, 0))


def recurrence():
    half = (filter_high - filter_low) / 2.0
    center = (filter_high + filter_low) / 2.0
    first = half / (filter_bottom - center)
    rows = [(1.0, 0.0, 0.0), (first / half, center, 0.0)]
    now = first
    for _ in range(APPLY - 1):
        later = 1.0 / (2.0 / first - now)
        rows.append((2.0 * later / half, center, now * later))
        now = later
    return np.asarray(rows, np.float32)


def side_of(step):
    return ORDER if step > 0 else 0


def dot_rows(a, b, precision=None):
    return lax.dot_general(
        a, b, (((0,), (0,)), ((), ())), precision=precision, preferred_element_type=jnp.float32
    )


def split(values):
    high = values.astype(jnp.bfloat16)
    return high, (values - high.astype(jnp.float32)).astype(jnp.bfloat16)


def groups(sizes, rows):
    for scattered in (("gy", "gz"), ("gz",)):
        count = int(np.prod([sizes[a] for a in scattered]))
        if rows % (16 * count) == 0:
            return scattered, tuple(a for a in AXES if a not in scattered)
    return (), AXES


def count_of(sizes, axes):
    return int(np.prod([sizes[a] for a in axes], dtype=np.int64))


def index_in(sizes, axes):
    index = 0
    for axis in axes:
        index = index * sizes[axis] + lax.axis_index(axis)
    return index


def device_at(sizes, axes, index):
    place = {axis: lax.axis_index(axis) for axis in AXES}
    for axis in reversed(axes):
        place[axis] = lax.rem(index, sizes[axis])
        index = index // sizes[axis]
    return tuple(place[axis] for axis in AXES)


def neighbour(sizes, step):
    return tuple(
        lax.rem(lax.axis_index(axis) + d + sizes[axis], sizes[axis]) for axis, d in zip(AXES, step)
    )


def greeted(sizes, all_axes):
    steps = {
        tuple(d % sizes[a] for a, d in zip(AXES, step))
        for step in Z_STEPS + X_STEPS + Y_STEPS + XY_STEPS
    }
    for axes in all_axes:
        for place in np.ndindex(*[sizes[a] for a in axes]):
            near = dict(zip(axes, place))
            steps.add(tuple(int(near.get(a, 0)) for a in AXES))
    steps.discard((0, 0, 0))
    return sorted(steps)


def exchange(sizes, axes, source, slots, send_sem, recv_sem):
    count = count_of(sizes, axes)
    me = index_in(sizes, axes)
    copies = []
    for r in range(1, count):
        place = lax.rem(me + r, count)
        copies.append(
            pltpu.make_async_remote_copy(
                src_ref=source(place),
                dst_ref=slots.at[me],
                send_sem=send_sem.at[r - 1],
                recv_sem=recv_sem.at[r - 1],
                device_id=device_at(sizes, axes, place),
                device_id_type=MESH,
            )
        )
    for copy in copies:
        copy.start()
    for copy in copies:
        copy.wait()


def sum_over_devices(sizes, part, scratch, finish, gathered):
    scattered, whole = groups(sizes, part.shape[0])
    if scattered:
        slots, send_sem, recv_sem = scratch[0]
        chunk = slots.shape[1]
        me = index_in(sizes, scattered)
        rows = lambda place: part.at[pl.ds(pl.multiple_of(place * chunk, chunk), chunk)]
        slots[me] = rows(me)[...]
        exchange(sizes, scattered, rows, slots, send_sem, recv_sem)
        total = jnp.sum(slots[...].astype(jnp.float32), axis=0)
    else:
        me = 0
        total = part[...].astype(jnp.float32)
    for axis, (slots, send_sem, recv_sem) in zip(whole, scratch[1:-1]):
        place = lax.axis_index(axis)
        slots[place] = total.astype(slots.dtype)
        exchange(sizes, (axis,), lambda _: slots.at[place], slots, send_sem, recv_sem)
        total = jnp.sum(slots[...].astype(jnp.float32), axis=0)
    gathered[me] = finish(total)
    if scattered:
        send_sem, recv_sem = scratch[-1]
        exchange(sizes, scattered, lambda _: gathered.at[me], gathered, send_sem, recv_sem)


def sum_scratch(sizes, rows, width, dtype=jnp.float32):
    scattered, whole = groups(sizes, rows)
    count = count_of(sizes, scattered)
    chunk = rows // count
    sems = lambda n: [pltpu.SemaphoreType.DMA((max(n - 1, 1),))] * 2
    shapes = [[pltpu.VMEM((count, chunk, width), dtype)] + sems(count)]
    for axis in whole:
        n = sizes[axis]
        shapes.append([pltpu.VMEM((n, chunk, width), dtype)] + sems(n))
    shapes.append(sems(count))
    return shapes


def merged(sizes):
    found = {}
    for step in XY_STEPS + X_STEPS + Y_STEPS:
        found.setdefault(tuple(d % sizes[a] for a, d in zip(AXES, step)), []).append(step)
    return list(found.values())


def part_rows(step, count):
    return count * TILE * (SIDE if 0 in step[:2] else 1)


class Halo:
    def __init__(self, sizes, cells, work, z_send, z_recv, f_send, f_recv, sems):
        self.sizes, self.cells, self.work = sizes, cells, work
        self.z_send, self.z_recv = z_send, z_recv
        self.f_send, self.f_recv = f_send, f_recv
        self.send_sem, self.recv_sem = sems
        self.messages = merged(sizes)
        steps = Z_STEPS + tuple(steps[0] for steps in self.messages)
        self.places = {step: neighbour(sizes, step) for step in steps}

    def remote(self, slot, number, step, source, target):
        return pltpu.make_async_remote_copy(
            src_ref=source,
            dst_ref=target,
            send_sem=self.send_sem.at[slot, number],
            recv_sem=self.recv_sem.at[slot, number],
            device_id=self.places[step],
            device_id_type=MESH,
        )

    def lines(self, cell, step):
        first = cell * CELL_ROWS
        if step[1] == 0:
            return [pl.ds(first + side_of(step[0]) * SIDE * TILE, SIDE * TILE)]
        if step[0] == 0:
            rows = range(SIDE)
        else:
            rows = [side_of(step[0])]
        return [pl.ds(first + (a * SIDE + side_of(step[1])) * TILE, TILE) for a in rows]

    def send_faces(self, slot, group, cells):
        copies = []
        row = 0
        for n, steps in enumerate(self.messages):
            begin = row
            for step in steps:
                part = [self.work[at, :] for k in cells for at in self.lines(k, step)]
                size = part_rows(step, len(cells))
                self.f_send[slot, group, row : row + size, :] = jnp.concatenate(part, 0).astype(
                    self.f_send.dtype
                )
                row += size
            rows = pl.ds(begin, row - begin)
            copies.append(
                self.remote(
                    slot,
                    len(Z_STEPS) + group * len(self.messages) + n,
                    steps[0],
                    self.f_send.at[slot, group, rows],
                    self.f_recv.at[slot, group, rows],
                )
            )
            copies[-1].start()
        return copies

    def add_faces(self, slot, group, cells, copies):
        row = 0
        for copy, steps in zip(copies, self.messages):
            copy.wait()
            for step in steps:
                size = part_rows(step, len(cells))
                got = self.f_recv[slot, group, row : row + size, :].astype(jnp.float32)
                row += size
                taken = 0
                for k in cells:
                    for at in self.lines(k, tuple(-d for d in step)):
                        self.work[at, :] = self.work[at, :] + got[taken : taken + at.size]
                        taken += at.size

    def z_rows(self, cell, c):
        return pl.ds(cell * CELL_ROWS + c, LINES, stride=TILE)

    def z_copies(self, slot):
        return [
            self.remote(slot, n, step, self.z_send.at[slot, n], self.z_recv.at[slot, n])
            for n, step in enumerate(Z_STEPS)
        ]

    def send_z(self, slot):
        work = self.work
        self.z_send[slot, 0] = work[self.z_rows(self.cells - 1, ORDER), :]
        self.z_send[slot, 1] = work[self.z_rows(0, 0), :]
        for copy in self.z_copies(slot):
            copy.start()
        for cell in range(self.cells - 1):
            lower, upper = self.z_rows(cell, ORDER), self.z_rows(cell + 1, 0)
            both = work[lower, :] + work[upper, :]
            work[lower, :] = both
            work[upper, :] = both

    def add_z(self, slot):
        work = self.work
        for copy in self.z_copies(slot):
            copy.wait()
        bottom, top = self.z_rows(0, 0), self.z_rows(self.cells - 1, ORDER)
        work[bottom, :] = work[bottom, :] + self.z_recv[slot, 0]
        work[top, :] = work[top, :] + self.z_recv[slot, 1]


def inverse_factor(gram, mixed, inverse):
    n = gram.shape[0]
    size = BLOCK_ROWS if n % BLOCK_ROWS == 0 else TILE
    mixed[...] = gram
    sub = lax.broadcasted_iota(jnp.int32, (size, n), 0)
    col = lax.broadcasted_iota(jnp.int32, (size, n), 1)
    for start in range(0, n, size):
        end = start + size
        rows = mixed[start:end, :]
        cols = [jnp.broadcast_to(rows[:, start + t : start + t + 1], (size, n)) for t in range(size)]
        unit = jnp.where(col - start == sub, 1.0, 0.0).astype(jnp.float32)
        rows = jnp.where((col >= start) & (col < end), unit, rows)
        scale = jnp.zeros((size, n), jnp.float32)
        for s in range(size):
            root = lax.rsqrt(cols[s][s : s + 1, :])
            scale = jnp.where(sub == s, root, scale)
            if s + 1 < size:
                ratio = jnp.where(sub > s, cols[s] * (root * root), 0.0)
                for t in range(s + 1, size):
                    cols[t] = cols[t] - ratio * cols[t][s : s + 1, :]
                rows = rows - ratio * rows[s : s + 1, :]
        rows = rows * scale
        inverse[start:end, :] = jnp.where(col < end, rows, 0.0)
        if end < n:
            change = dot_rows(jnp.where(col >= end, rows, 0.0), rows, HIGHEST)[end:, :]
            rest = lax.broadcasted_iota(jnp.int32, (n - end, n), 1)
            kept = jnp.where((rest >= start) & (rest < end), 0.0, mixed[end:, :])
            mixed[end:, :] = kept - change


def kernel(
    sizes,
    cells,
    nodes_total,
    coef_ref,
    start_ref,
    locked_ref,
    h_ref,
    parts,
    gram_rows,
    padded_h,
    grid_nodes,
    state,
    work,
    z_send,
    z_recv,
    f_send,
    f_recv,
    halo_sems,
    locked_t,
    cross_part,
    cross_scratch,
    coefficient,
    gram_part,
    gram_scratch,
):
    width = work.shape[1]
    node = h_ref.shape[1]
    steps = greeted(sizes, [groups(sizes, locked_ref.shape[1])[0], groups(sizes, width)[0], *[(a,) for a in AXES]])
    barrier = pltpu.get_barrier_semaphore()
    for step in steps:
        pl.semaphore_signal(
            barrier, inc=1, device_id=neighbour(sizes, step), device_id_type=MESH
        )

    own = start_ref.shape[2]
    grid_nodes[...] = jnp.zeros_like(grid_nodes)
    grid_nodes[:, :, :own, :] = start_ref[...].astype(jnp.float32)
    work[...] = jnp.zeros_like(work)
    sub = lax.broadcasted_iota(jnp.int32, (ORDER, TILE, width), 1)
    for k in range(cells):
        for a in range(ORDER):
            values = grid_nodes[a, :, ORDER * k : ORDER * k + TILE, :]
            first = k * CELL_ROWS + a * SIDE * TILE
            work[first : first + ORDER * TILE, :] = jnp.where(sub < ORDER, values, 0.0).reshape(
                ORDER * TILE, width
            )
    pl.semaphore_wait(barrier, len(steps))
    halo = Halo(sizes, cells, work, z_send, z_recv, f_send, f_recv, halo_sems)
    inner, outer = tuple(range(1, cells - 1)), (0, cells - 1)
    state[...] = jnp.zeros(state.shape, jnp.float32)

    def finish_faces(slot, inner_copies, outer_copies):
        halo.add_faces(slot, 0, inner, inner_copies)
        halo.add_faces(slot, 1, outer, outer_copies)
        halo.send_z(slot)

    def update(t, group):
        now, old = lax.rem(t, 2), lax.rem(t + 1, 2)
        scale, shift, back = coef_ref[t, 0], coef_ref[t, 1], coef_ref[t, 2]
        for k in group:
            rows = pl.ds(k * CELL_ROWS, CELL_ROWS)
            state[now, rows, :] = (
                scale * (work[rows, :] - shift * state[old, rows, :]) - back * state[now, rows, :]
            )

    def multiply(t, group):
        for k in group:
            rows = pl.ds(k * CELL_ROWS, CELL_ROWS)
            values = state[lax.rem(t, 2), rows, :].astype(jnp.bfloat16)
            work[rows, :] = jnp.dot(padded_h[k], values, preferred_element_type=jnp.float32)

    inner_copies = halo.send_faces(0, 0, inner)
    outer_copies = halo.send_faces(0, 1, outer)
    row = lax.broadcasted_iota(jnp.int32, (CELL_ROWS, node), 0)
    col = lax.broadcasted_iota(jnp.int32, (CELL_ROWS, node), 1)
    place = jnp.where(row % TILE < SIDE, row // TILE * SIDE + row % TILE, -1)
    spread = jnp.where(col == place, 1.0, 0.0).astype(jnp.bfloat16)
    for k in range(cells):
        tall = jnp.dot(spread, h_ref[k], preferred_element_type=jnp.float32).astype(jnp.bfloat16)
        padded_h[k] = lax.dot_general(
            tall, spread, (((1,), (1,)), ((), ())), preferred_element_type=jnp.float32
        ).astype(jnp.bfloat16)
    locked_t[...] = locked_ref[...].T
    finish_faces(0, inner_copies, outer_copies)

    def apply(t, carry):
        slot = lax.rem(t, 2)
        update(t - 1, inner)
        multiply(t - 1, inner)
        inner_copies = halo.send_faces(slot, 0, inner)
        halo.add_z(lax.rem(t - 1, 2))
        update(t - 1, outer)
        multiply(t - 1, outer)
        outer_copies = halo.send_faces(slot, 1, outer)
        finish_faces(slot, inner_copies, outer_copies)
        return carry

    lax.fori_loop(1, APPLY + 1, apply, 0)
    update(APPLY, inner)
    halo.add_z(APPLY % 2)
    update(APPLY, outer)
    last = APPLY % 2
    for k in range(cells):
        for a in range(ORDER):
            first = k * CELL_ROWS + a * SIDE * TILE
            grid_nodes[a, :, ORDER * k : ORDER * k + TILE, :] = state[
                last, first : first + ORDER * TILE, :
            ].reshape(ORDER, TILE, width)
    filtered = (
        grid_nodes[:, :, :own, :].reshape(ORDER * ORDER * own, width).astype(jnp.bfloat16)
    )
    cross_part[...] = jnp.dot(
        locked_t[...], filtered, preferred_element_type=jnp.float32
    ).astype(cross_part.dtype)
    sum_over_devices(
        sizes,
        cross_part,
        cross_scratch,
        lambda total: (total / nodes_total).astype(jnp.bfloat16),
        coefficient,
    )
    projected = filtered.astype(jnp.float32) - jnp.dot(
        locked_ref[...],
        coefficient[...].reshape(locked_ref.shape[1], width),
        preferred_element_type=jnp.float32,
    )
    high, low = split(projected)
    parts[:, :width] = high
    parts[:, width:] = low
    terms = dot_rows(parts[...], parts[...])
    gram_part[...] = (
        terms[:width, :width]
        + (terms[:width, width:] + terms[width:, :width])
        + terms[width:, width:]
    )
    sum_over_devices(sizes, gram_part, gram_scratch, lambda total: total / nodes_total, gram_rows)


def finish_kernel(parts, gram_rows, out_ref, mixed, inverse):
    width = out_ref.shape[1]
    inverse_factor(gram_rows[...].reshape(width, width), mixed, inverse)
    inverse_high, inverse_low = split(inverse[...])
    wide = jnp.concatenate([inverse_high, inverse_high], axis=1)
    contract = (((1,), (1,)), ((), ()))
    out_ref[...] = lax.dot_general(
        parts[...], wide, contract, preferred_element_type=jnp.float32
    ) + lax.dot_general(
        parts[:, :width], inverse_low, contract, preferred_element_type=jnp.float32
    )


def per_device(sizes, start_block, locked_orbitals, cell_h):
    width = start_block.shape[3]
    locked = locked_orbitals.shape[3]
    own = start_block.shape[2]
    cells = cell_h.shape[2]
    assert cell_h.shape[:2] == (1, 1)
    nodes = ORDER * ORDER * own
    nodes_total = float(nodes * count_of(sizes, AXES))
    count = lambda rows: count_of(sizes, groups(sizes, rows)[0])
    largest = max(cells - 2, 2)
    faces = sum(part_rows(step, largest) for step in X_STEPS + Y_STEPS + XY_STEPS)
    messages = len(Z_STEPS) + 2 * len(merged(sizes))
    vmem = pltpu.VMEM
    scratch = [
        vmem((cells, CELL_ROWS, CELL_ROWS), jnp.bfloat16),
        vmem((ORDER, ORDER, own + TILE, width), jnp.float32),
        vmem((2, cells * CELL_ROWS, width), jnp.float32),
        vmem((cells * CELL_ROWS, width), jnp.float32),
        vmem((2, 2, LINES, width), jnp.float32),
        vmem((2, 2, LINES, width), jnp.float32),
        vmem((2, 2, faces, width), jnp.bfloat16),
        vmem((2, 2, faces, width), jnp.bfloat16),
        [pltpu.SemaphoreType.DMA((2, messages))] * 2,
        vmem((locked, nodes), jnp.bfloat16),
        vmem((locked, width), jnp.bfloat16),
        sum_scratch(sizes, locked, width, jnp.bfloat16),
        vmem((count(locked), locked // count(locked), width), jnp.bfloat16),
        vmem((width, width), jnp.float32),
        sum_scratch(sizes, width, width),
    ]
    block = pl.BlockSpec(memory_space=pltpu.VMEM)
    parts, gram = pl.pallas_call(
        functools.partial(kernel, sizes, cells, nodes_total),
        out_shape=(
            jax.ShapeDtypeStruct((nodes, 2 * width), jnp.bfloat16),
            jax.ShapeDtypeStruct((count(width), width // count(width), width), jnp.float32),
        ),
        in_specs=[pl.BlockSpec(memory_space=pltpu.SMEM)]
        + [block] * 3,
        out_specs=(block, block),
        scratch_shapes=scratch,
        compiler_params=pltpu.CompilerParams(
            collective_id=0, has_side_effects=True, vmem_limit_bytes=40 << 20
        ),
    )(
        jnp.asarray(recurrence()),
        start_block,
        locked_orbitals.reshape(nodes, locked),
        cell_h.reshape(cell_h.shape[2:]),
    )
    result = pl.pallas_call(
        finish_kernel,
        out_shape=jax.ShapeDtypeStruct((nodes, width), jnp.float32),
        in_specs=[block, block],
        out_specs=block,
        scratch_shapes=[vmem((width, width), jnp.float32), vmem((width, width), jnp.float32)],
        compiler_params=pltpu.CompilerParams(vmem_limit_bytes=16 << 20),
    )(parts, gram)
    return result.reshape(start_block.shape)


def solution(mesh):
    sizes = dict(mesh.shape)
    placed = (P("gx", "gy", "gz", None), P("gx", "gy", "gz", None), P("gx", "gy", "gz", None, None))
    return jax.shard_map(
        functools.partial(per_device, sizes),
        mesh=mesh,
        in_specs=placed,
        out_specs=P("gx", "gy", "gz", None),
        check_vma=False,
    )
```

```python
import functools

import jax
import jax.numpy as jnp
import numpy as np
from jax import lax
from jax.experimental import pallas as pl
from jax.experimental.pallas import tpu as pltpu
from jax.sharding import PartitionSpec as P

ORDER = 6
SIDE = ORDER + 1
TILE = 8
LINES = SIDE * SIDE
CELL_ROWS = LINES * TILE
APPLY = 6
BLOCK_ROWS = 16
AXES = ("gx", "gy", "gz")

filter_low = 3.0
filter_high = 40.0
filter_bottom = 0.5

MESH = pl.DeviceIdType.MESH
HIGHEST = lax.Precision.HIGHEST

Z_STEPS = ((0, 0, 1), (0, 0, -1))
X_STEPS = ((1, 0, 0), (-1, 0, 0))
Y_STEPS = ((0, 1, 0), (0, -1, 0))
XY_STEPS = ((1, 1, 0), (1, -1, 0), (-1, 1, 0), (-1, -1, 0))


def recurrence():
    half = (filter_high - filter_low) / 2.0
    center = (filter_high + filter_low) / 2.0
    first = half / (filter_bottom - center)
    rows = [(1.0, 0.0, 0.0), (first / half, center, 0.0)]
    now = first
    for _ in range(APPLY - 1):
        later = 1.0 / (2.0 / first - now)
        rows.append((2.0 * later / half, center, now * later))
        now = later
    return np.asarray(rows, np.float32)


def side_of(step):
    return ORDER if step > 0 else 0


def dot_rows(a, b, precision=None):
    return lax.dot_general(
        a, b, (((0,), (0,)), ((), ())), precision=precision, preferred_element_type=jnp.float32
    )


def split(values):
    high = values.astype(jnp.bfloat16)
    return high, (values - high.astype(jnp.float32)).astype(jnp.bfloat16)


def groups(sizes, rows):
    for scattered in (("gy", "gz"), ("gz",)):
        count = int(np.prod([sizes[a] for a in scattered]))
        if rows % (16 * count) == 0:
            return scattered, tuple(a for a in AXES if a not in scattered)
    return (), AXES


def count_of(sizes, axes):
    return int(np.prod([sizes[a] for a in axes], dtype=np.int64))


def index_in(sizes, axes):
    index = 0
    for axis in axes:
        index = index * sizes[axis] + lax.axis_index(axis)
    return index


def device_at(sizes, axes, index):
    place = {axis: lax.axis_index(axis) for axis in AXES}
    for axis in reversed(axes):
        place[axis] = lax.rem(index, sizes[axis])
        index = index // sizes[axis]
    return tuple(place[axis] for axis in AXES)


def neighbour(sizes, step):
    return tuple(
        lax.rem(lax.axis_index(axis) + d + sizes[axis], sizes[axis]) for axis, d in zip(AXES, step)
    )


def greeted(sizes, all_axes):
    steps = {
        tuple(d % sizes[a] for a, d in zip(AXES, step))
        for step in Z_STEPS + X_STEPS + Y_STEPS + XY_STEPS
    }
    for axes in all_axes:
        for place in np.ndindex(*[sizes[a] for a in axes]):
            near = dict(zip(axes, place))
            steps.add(tuple(int(near.get(a, 0)) for a in AXES))
    steps.discard((0, 0, 0))
    return sorted(steps)


def exchange(sizes, axes, source, slots, send_sem, recv_sem):
    count = count_of(sizes, axes)
    me = index_in(sizes, axes)
    copies = []
    for r in range(1, count):
        place = lax.rem(me + r, count)
        copies.append(
            pltpu.make_async_remote_copy(
                src_ref=source(place),
                dst_ref=slots.at[me],
                send_sem=send_sem.at[r - 1],
                recv_sem=recv_sem.at[r - 1],
                device_id=device_at(sizes, axes, place),
                device_id_type=MESH,
            )
        )
    for copy in copies:
        copy.start()
    for copy in copies:
        copy.wait()


def sum_over_devices(sizes, part, scratch, finish, gathered):
    scattered, whole = groups(sizes, part.shape[0])
    if scattered:
        slots, send_sem, recv_sem = scratch[0]
        chunk = slots.shape[1]
        me = index_in(sizes, scattered)
        rows = lambda place: part.at[pl.ds(pl.multiple_of(place * chunk, chunk), chunk)]
        slots[me] = rows(me)[...]
        exchange(sizes, scattered, rows, slots, send_sem, recv_sem)
        total = jnp.sum(slots[...].astype(jnp.float32), axis=0)
    else:
        me = 0
        total = part[...].astype(jnp.float32)
    for axis, (slots, send_sem, recv_sem) in zip(whole, scratch[1:-1]):
        place = lax.axis_index(axis)
        slots[place] = total.astype(slots.dtype)
        exchange(sizes, (axis,), lambda _: slots.at[place], slots, send_sem, recv_sem)
        total = jnp.sum(slots[...].astype(jnp.float32), axis=0)
    gathered[me] = finish(total)
    if scattered:
        send_sem, recv_sem = scratch[-1]
        exchange(sizes, scattered, lambda _: gathered.at[me], gathered, send_sem, recv_sem)


def sum_scratch(sizes, rows, width, dtype=jnp.float32):
    scattered, whole = groups(sizes, rows)
    count = count_of(sizes, scattered)
    chunk = rows // count
    sems = lambda n: [pltpu.SemaphoreType.DMA((max(n - 1, 1),))] * 2
    shapes = [[pltpu.VMEM((count, chunk, width), dtype)] + sems(count)]
    for axis in whole:
        n = sizes[axis]
        shapes.append([pltpu.VMEM((n, chunk, width), dtype)] + sems(n))
    shapes.append(sems(count))
    return shapes


def merged(sizes, wanted=lambda step: True):
    found = {}
    for step in filter(wanted, XY_STEPS + X_STEPS + Y_STEPS):
        found.setdefault(tuple(d % sizes[a] for a, d in zip(AXES, step)), []).append(step)
    return list(found.values())


def part_rows(step, count):
    return count * TILE * (SIDE if 0 in step[:2] else 1)


class Halo:
    def __init__(self, sizes, cells, work, z_send, z_recv, f_send, f_recv, sems):
        self.sizes, self.cells, self.work = sizes, cells, work
        self.z_send, self.z_recv = z_send, z_recv
        self.f_send, self.f_recv = f_send, f_recv
        self.send_sem, self.recv_sem = sems
        self.messages = merged(sizes)
        self.down = merged(sizes, lambda step: max(step) <= 0)
        self.up = merged(sizes, lambda step: min(step) >= 0)
        steps = Z_STEPS + tuple(m[0] for m in self.messages + self.down + self.up)
        self.places = {step: neighbour(sizes, step) for step in steps}

    def remote(self, slot, number, step, source, target):
        return pltpu.make_async_remote_copy(
            src_ref=source,
            dst_ref=target,
            send_sem=self.send_sem.at[slot, number],
            recv_sem=self.recv_sem.at[slot, number],
            device_id=self.places[step],
            device_id_type=MESH,
        )

    def lines(self, cell, step):
        first = cell * CELL_ROWS
        if step[1] == 0:
            return [pl.ds(first + side_of(step[0]) * SIDE * TILE, SIDE * TILE)]
        if step[0] == 0:
            rows = range(SIDE)
        else:
            rows = [side_of(step[0])]
        return [pl.ds(first + (a * SIDE + side_of(step[1])) * TILE, TILE) for a in rows]

    def send_faces(self, slot, group, cells, messages):
        copies = []
        row = 0
        for n, steps in enumerate(messages):
            begin = row
            for step in steps:
                part = [self.work[at, :] for k in cells for at in self.lines(k, step)]
                size = part_rows(step, len(cells))
                self.f_send[slot, group, row : row + size, :] = jnp.concatenate(part, 0).astype(
                    self.f_send.dtype
                )
                row += size
            rows = pl.ds(begin, row - begin)
            copies.append(
                self.remote(
                    slot,
                    len(Z_STEPS) + group * len(self.messages) + n,
                    steps[0],
                    self.f_send.at[slot, group, rows],
                    self.f_recv.at[slot, group, rows],
                )
            )
            copies[-1].start()
        return copies

    def add_faces(self, slot, group, cells, copies, messages):
        row = 0
        for copy, steps in zip(copies, messages):
            copy.wait()
            for step in steps:
                size = part_rows(step, len(cells))
                got = self.f_recv[slot, group, row : row + size, :].astype(jnp.float32)
                row += size
                taken = 0
                for k in cells:
                    for at in self.lines(k, tuple(-d for d in step)):
                        self.work[at, :] = self.work[at, :] + got[taken : taken + at.size]
                        taken += at.size

    def z_rows(self, cell, c):
        return pl.ds(cell * CELL_ROWS + c, LINES, stride=TILE)

    def z_copies(self, slot):
        return [
            self.remote(slot, n, step, self.z_send.at[slot, n], self.z_recv.at[slot, n])
            for n, step in enumerate(Z_STEPS)
        ]

    def send_z(self, slot):
        work = self.work
        self.z_send[slot, 0] = work[self.z_rows(self.cells - 1, ORDER), :]
        self.z_send[slot, 1] = work[self.z_rows(0, 0), :]
        for copy in self.z_copies(slot):
            copy.start()
        for cell in range(self.cells - 1):
            lower, upper = self.z_rows(cell, ORDER), self.z_rows(cell + 1, 0)
            both = work[lower, :] + work[upper, :]
            work[lower, :] = both
            work[upper, :] = both

    def add_z(self, slot):
        work = self.work
        for copy in self.z_copies(slot):
            copy.wait()
        bottom, top = self.z_rows(0, 0), self.z_rows(self.cells - 1, ORDER)
        work[bottom, :] = work[bottom, :] + self.z_recv[slot, 0]
        work[top, :] = work[top, :] + self.z_recv[slot, 1]


def inverse_factor(gram, mixed, inverse):
    n = gram.shape[0]
    size = BLOCK_ROWS if n % BLOCK_ROWS == 0 else TILE
    mixed[...] = gram
    sub = lax.broadcasted_iota(jnp.int32, (size, n), 0)
    col = lax.broadcasted_iota(jnp.int32, (size, n), 1)
    for start in range(0, n, size):
        end = start + size
        rows = mixed[start:end, :]
        cols = [jnp.broadcast_to(rows[:, start + t : start + t + 1], (size, n)) for t in range(size)]
        unit = jnp.where(col - start == sub, 1.0, 0.0).astype(jnp.float32)
        rows = jnp.where((col >= start) & (col < end), unit, rows)
        scale = jnp.zeros((size, n), jnp.float32)
        for s in range(size):
            root = lax.rsqrt(cols[s][s : s + 1, :])
            scale = jnp.where(sub == s, root, scale)
            if s + 1 < size:
                ratio = jnp.where(sub > s, cols[s] * (root * root), 0.0)
                for t in range(s + 1, size):
                    cols[t] = cols[t] - ratio * cols[t][s : s + 1, :]
                rows = rows - ratio * rows[s : s + 1, :]
        rows = rows * scale
        inverse[start:end, :] = jnp.where(col < end, rows, 0.0)
        if end < n:
            change = dot_rows(jnp.where(col >= end, rows, 0.0), rows, HIGHEST)[end:, :]
            rest = lax.broadcasted_iota(jnp.int32, (n - end, n), 1)
            kept = jnp.where((rest >= start) & (rest < end), 0.0, mixed[end:, :])
            mixed[end:, :] = kept - change


def kernel(
    sizes,
    cells,
    nodes_total,
    coef_ref,
    start_ref,
    locked_ref,
    h_ref,
    parts,
    gram_rows,
    padded_h,
    grid_nodes,
    state,
    work,
    z_send,
    z_recv,
    f_send,
    f_recv,
    halo_sems,
    locked_t,
    cross_part,
    cross_scratch,
    coefficient,
    gram_part,
    gram_scratch,
):
    width = work.shape[1]
    node = h_ref.shape[1]
    steps = greeted(sizes, [groups(sizes, locked_ref.shape[1])[0], groups(sizes, width)[0], *[(a,) for a in AXES]])
    barrier = pltpu.get_barrier_semaphore()
    for step in steps:
        pl.semaphore_signal(
            barrier, inc=1, device_id=neighbour(sizes, step), device_id_type=MESH
        )

    own = start_ref.shape[2]
    grid_nodes[...] = jnp.zeros_like(grid_nodes)
    grid_nodes[:, :, :own, :] = start_ref[...].astype(jnp.float32)
    work[...] = jnp.zeros_like(work)
    sub = lax.broadcasted_iota(jnp.int32, (ORDER, TILE, width), 1)
    for k in range(cells):
        for a in range(ORDER):
            values = grid_nodes[a, :, ORDER * k : ORDER * k + TILE, :]
            first = k * CELL_ROWS + a * SIDE * TILE
            work[first : first + ORDER * TILE, :] = jnp.where(sub < ORDER, values, 0.0).reshape(
                ORDER * TILE, width
            )
    pl.semaphore_wait(barrier, len(steps))
    halo = Halo(sizes, cells, work, z_send, z_recv, f_send, f_recv, halo_sems)
    inner, outer = tuple(range(1, cells - 1)), (0, cells - 1)
    state[...] = jnp.zeros(state.shape, jnp.float32)

    def finish_faces(slot, inner_copies, outer_copies, messages):
        halo.add_faces(slot, 0, inner, inner_copies, messages)
        halo.add_faces(slot, 1, outer, outer_copies, messages)
        halo.send_z(slot)

    def update(t, group):
        now, old = lax.rem(t, 2), lax.rem(t + 1, 2)
        scale, shift, back = coef_ref[t, 0], coef_ref[t, 1], coef_ref[t, 2]
        for k in group:
            rows = pl.ds(k * CELL_ROWS, CELL_ROWS)
            state[now, rows, :] = (
                scale * (work[rows, :] - shift * state[old, rows, :]) - back * state[now, rows, :]
            )

    def multiply(t, group):
        for k in group:
            rows = pl.ds(k * CELL_ROWS, CELL_ROWS)
            values = state[lax.rem(t, 2), rows, :].astype(jnp.bfloat16)
            work[rows, :] = jnp.dot(padded_h[k], values, preferred_element_type=jnp.float32)

    inner_copies = halo.send_faces(0, 0, inner, halo.down)
    outer_copies = halo.send_faces(0, 1, outer, halo.down)
    row = lax.broadcasted_iota(jnp.int32, (CELL_ROWS, node), 0)
    col = lax.broadcasted_iota(jnp.int32, (CELL_ROWS, node), 1)
    place = jnp.where(row % TILE < SIDE, row // TILE * SIDE + row % TILE, -1)
    spread = jnp.where(col == place, 1.0, 0.0).astype(jnp.bfloat16)
    for k in range(cells):
        tall = jnp.dot(spread, h_ref[k], preferred_element_type=jnp.float32).astype(jnp.bfloat16)
        padded_h[k] = lax.dot_general(
            tall, spread, (((1,), (1,)), ((), ())), preferred_element_type=jnp.float32
        ).astype(jnp.bfloat16)
    locked_t[...] = locked_ref[...].T
    finish_faces(0, inner_copies, outer_copies, halo.down)

    def apply(t, messages):
        slot = lax.rem(t, 2)
        update(t - 1, inner)
        multiply(t - 1, inner)
        inner_copies = halo.send_faces(slot, 0, inner, messages)
        halo.add_z(lax.rem(t - 1, 2))
        update(t - 1, outer)
        multiply(t - 1, outer)
        outer_copies = halo.send_faces(slot, 1, outer, messages)
        finish_faces(slot, inner_copies, outer_copies, messages)

    def repeat(t, carry):
        apply(t, halo.messages)
        return carry

    lax.fori_loop(1, APPLY, repeat, 0)
    apply(APPLY, halo.up)
    update(APPLY, inner)
    halo.add_z(APPLY % 2)
    update(APPLY, outer)
    last = APPLY % 2
    for k in range(cells):
        for a in range(ORDER):
            first = k * CELL_ROWS + a * SIDE * TILE
            grid_nodes[a, :, ORDER * k : ORDER * k + TILE, :] = state[
                last, first : first + ORDER * TILE, :
            ].reshape(ORDER, TILE, width)
    filtered = (
        grid_nodes[:, :, :own, :].reshape(ORDER * ORDER * own, width).astype(jnp.bfloat16)
    )
    cross_part[...] = jnp.dot(
        locked_t[...], filtered, preferred_element_type=jnp.float32
    ).astype(cross_part.dtype)
    sum_over_devices(
        sizes,
        cross_part,
        cross_scratch,
        lambda total: (total / nodes_total).astype(jnp.bfloat16),
        coefficient,
    )
    projected = filtered.astype(jnp.float32) - jnp.dot(
        locked_ref[...],
        coefficient[...].reshape(locked_ref.shape[1], width),
        preferred_element_type=jnp.float32,
    )
    high, low = split(projected)
    parts[:, :width] = high
    parts[:, width:] = low
    terms = dot_rows(parts[...], parts[...])
    gram_part[...] = (
        terms[:width, :width]
        + (terms[:width, width:] + terms[width:, :width])
        + terms[width:, width:]
    )
    sum_over_devices(sizes, gram_part, gram_scratch, lambda total: total / nodes_total, gram_rows)


def finish_kernel(parts, gram_rows, out_ref, mixed, inverse):
    width = out_ref.shape[1]
    inverse_factor(gram_rows[...].reshape(width, width), mixed, inverse)
    inverse_high, inverse_low = split(inverse[...])
    wide = jnp.concatenate([inverse_high, inverse_high], axis=1)
    contract = (((1,), (1,)), ((), ()))
    out_ref[...] = lax.dot_general(
        parts[...], wide, contract, preferred_element_type=jnp.float32
    ) + lax.dot_general(
        parts[:, :width], inverse_low, contract, preferred_element_type=jnp.float32
    )


def per_device(sizes, start_block, locked_orbitals, cell_h):
    width = start_block.shape[3]
    locked = locked_orbitals.shape[3]
    own = start_block.shape[2]
    cells = cell_h.shape[2]
    assert cell_h.shape[:2] == (1, 1)
    nodes = ORDER * ORDER * own
    nodes_total = float(nodes * count_of(sizes, AXES))
    count = lambda rows: count_of(sizes, groups(sizes, rows)[0])
    largest = max(cells - 2, 2)
    faces = sum(part_rows(step, largest) for step in X_STEPS + Y_STEPS + XY_STEPS)
    messages = len(Z_STEPS) + 2 * len(merged(sizes))
    vmem = pltpu.VMEM
    scratch = [
        vmem((cells, CELL_ROWS, CELL_ROWS), jnp.bfloat16),
        vmem((ORDER, ORDER, own + TILE, width), jnp.float32),
        vmem((2, cells * CELL_ROWS, width), jnp.float32),
        vmem((cells * CELL_ROWS, width), jnp.float32),
        vmem((2, 2, LINES, width), jnp.float32),
        vmem((2, 2, LINES, width), jnp.float32),
        vmem((2, 2, faces, width), jnp.bfloat16),
        vmem((2, 2, faces, width), jnp.bfloat16),
        [pltpu.SemaphoreType.DMA((2, messages))] * 2,
        vmem((locked, nodes), jnp.bfloat16),
        vmem((locked, width), jnp.bfloat16),
        sum_scratch(sizes, locked, width, jnp.bfloat16),
        vmem((count(locked), locked // count(locked), width), jnp.bfloat16),
        vmem((width, width), jnp.float32),
        sum_scratch(sizes, width, width),
    ]
    block = pl.BlockSpec(memory_space=pltpu.VMEM)
    parts, gram = pl.pallas_call(
        functools.partial(kernel, sizes, cells, nodes_total),
        out_shape=(
            jax.ShapeDtypeStruct((nodes, 2 * width), jnp.bfloat16),
            jax.ShapeDtypeStruct((count(width), width // count(width), width), jnp.float32),
        ),
        in_specs=[pl.BlockSpec(memory_space=pltpu.SMEM)]
        + [block] * 3,
        out_specs=(block, block),
        scratch_shapes=scratch,
        compiler_params=pltpu.CompilerParams(
            collective_id=0, has_side_effects=True, vmem_limit_bytes=40 << 20
        ),
    )(
        jnp.asarray(recurrence()),
        start_block,
        locked_orbitals.reshape(nodes, locked),
        cell_h.reshape(cell_h.shape[2:]),
    )
    result = pl.pallas_call(
        finish_kernel,
        out_shape=jax.ShapeDtypeStruct((nodes, width), jnp.float32),
        in_specs=[block, block],
        out_specs=block,
        scratch_shapes=[vmem((width, width), jnp.float32), vmem((width, width), jnp.float32)],
        compiler_params=pltpu.CompilerParams(vmem_limit_bytes=16 << 20),
    )(parts, gram)
    return result.reshape(start_block.shape)


def solution(mesh):
    sizes = dict(mesh.shape)
    placed = (P("gx", "gy", "gz", None), P("gx", "gy", "gz", None), P("gx", "gy", "gz", None, None))
    return jax.shard_map(
        functools.partial(per_device, sizes),
        mesh=mesh,
        in_specs=placed,
        out_specs=P("gx", "gy", "gz", None),
        check_vma=False,
    )
```

```python
import functools

import jax
import jax.numpy as jnp
import numpy as np
from jax import lax
from jax.experimental import pallas as pl
from jax.experimental.pallas import tpu as pltpu
from jax.sharding import PartitionSpec as P

ORDER = 6
SIDE = ORDER + 1
TILE = 8
LINES = SIDE * SIDE
CELL_ROWS = LINES * TILE
APPLY = 6
BLOCK_ROWS = 16
AXES = ("gx", "gy", "gz")

filter_low = 3.0
filter_high = 40.0
filter_bottom = 0.5

MESH = pl.DeviceIdType.MESH
HIGHEST = lax.Precision.HIGHEST

Z_STEPS = ((0, 0, 1), (0, 0, -1))
X_STEPS = ((1, 0, 0), (-1, 0, 0))
Y_STEPS = ((0, 1, 0), (0, -1, 0))
XY_STEPS = ((1, 1, 0), (1, -1, 0), (-1, 1, 0), (-1, -1, 0))


def recurrence():
    half = (filter_high - filter_low) / 2.0
    center = (filter_high + filter_low) / 2.0
    first = half / (filter_bottom - center)
    rows = [(1.0, 0.0, 0.0), (first / half, center, 0.0)]
    now = first
    for _ in range(APPLY - 1):
        later = 1.0 / (2.0 / first - now)
        rows.append((2.0 * later / half, center, now * later))
        now = later
    return np.asarray(rows, np.float32)


def side_of(step):
    return ORDER if step > 0 else 0


def dot_rows(a, b, precision=None):
    return lax.dot_general(
        a, b, (((0,), (0,)), ((), ())), precision=precision, preferred_element_type=jnp.float32
    )


def split(values):
    high = values.astype(jnp.bfloat16)
    return high, (values - high.astype(jnp.float32)).astype(jnp.bfloat16)


def groups(sizes, rows):
    for scattered in (("gy", "gz"), ("gz",)):
        count = int(np.prod([sizes[a] for a in scattered]))
        if rows % (16 * count) == 0:
            return scattered, tuple(a for a in AXES if a not in scattered)
    return (), AXES


def count_of(sizes, axes):
    return int(np.prod([sizes[a] for a in axes], dtype=np.int64))


def index_in(sizes, axes):
    index = 0
    for axis in axes:
        index = index * sizes[axis] + lax.axis_index(axis)
    return index


def device_at(sizes, axes, index):
    place = {axis: lax.axis_index(axis) for axis in AXES}
    for axis in reversed(axes):
        place[axis] = lax.rem(index, sizes[axis])
        index = index // sizes[axis]
    return tuple(place[axis] for axis in AXES)


def neighbour(sizes, step):
    return tuple(
        lax.rem(lax.axis_index(axis) + d + sizes[axis], sizes[axis]) for axis, d in zip(AXES, step)
    )


def greeted(sizes, all_axes):
    steps = {
        tuple(d % sizes[a] for a, d in zip(AXES, step))
        for step in Z_STEPS + X_STEPS + Y_STEPS + XY_STEPS
    }
    for axes in all_axes:
        for place in np.ndindex(*[sizes[a] for a in axes]):
            near = dict(zip(axes, place))
            steps.add(tuple(int(near.get(a, 0)) for a in AXES))
    steps.discard((0, 0, 0))
    return sorted(steps)


def exchange(sizes, axes, source, slots, send_sem, recv_sem):
    count = count_of(sizes, axes)
    me = index_in(sizes, axes)
    copies = []
    for r in range(1, count):
        place = lax.rem(me + r, count)
        copies.append(
            pltpu.make_async_remote_copy(
                src_ref=source(place),
                dst_ref=slots.at[me],
                send_sem=send_sem.at[r - 1],
                recv_sem=recv_sem.at[r - 1],
                device_id=device_at(sizes, axes, place),
                device_id_type=MESH,
            )
        )
    for copy in copies:
        copy.start()
    for copy in copies:
        copy.wait()


def sum_over_devices(sizes, part, scratch, finish, gathered):
    scattered, whole = groups(sizes, part.shape[0])
    if scattered:
        slots, send_sem, recv_sem = scratch[0]
        chunk = slots.shape[1]
        me = index_in(sizes, scattered)
        rows = lambda place: part.at[pl.ds(pl.multiple_of(place * chunk, chunk), chunk)]
        slots[me] = rows(me)[...]
        exchange(sizes, scattered, rows, slots, send_sem, recv_sem)
        total = jnp.sum(slots[...].astype(jnp.float32), axis=0)
    else:
        me = 0
        total = part[...].astype(jnp.float32)
    for axis, (slots, send_sem, recv_sem) in zip(whole, scratch[1:-1]):
        place = lax.axis_index(axis)
        slots[place] = total.astype(slots.dtype)
        exchange(sizes, (axis,), lambda _: slots.at[place], slots, send_sem, recv_sem)
        total = jnp.sum(slots[...].astype(jnp.float32), axis=0)
    gathered[me] = finish(total)
    if scattered:
        send_sem, recv_sem = scratch[-1]
        exchange(sizes, scattered, lambda _: gathered.at[me], gathered, send_sem, recv_sem)


def sum_scratch(sizes, rows, width, dtype=jnp.float32):
    scattered, whole = groups(sizes, rows)
    count = count_of(sizes, scattered)
    chunk = rows // count
    sems = lambda n: [pltpu.SemaphoreType.DMA((max(n - 1, 1),))] * 2
    shapes = [[pltpu.VMEM((count, chunk, width), dtype)] + sems(count)]
    for axis in whole:
        n = sizes[axis]
        shapes.append([pltpu.VMEM((n, chunk, width), dtype)] + sems(n))
    shapes.append(sems(count))
    return shapes


def merged(sizes, wanted=lambda step: True):
    found = {}
    for step in filter(wanted, XY_STEPS + X_STEPS + Y_STEPS):
        found.setdefault(tuple(d % sizes[a] for a, d in zip(AXES, step)), []).append(step)
    return list(found.values())


def part_rows(step, count):
    return count * TILE * (SIDE if 0 in step[:2] else 1)


class Halo:
    def __init__(self, sizes, cells, work, z_send, z_recv, f_send, f_recv, sems):
        self.sizes, self.cells, self.work = sizes, cells, work
        self.z_send, self.z_recv = z_send, z_recv
        self.f_send, self.f_recv = f_send, f_recv
        self.send_sem, self.recv_sem = sems
        self.messages = merged(sizes)
        self.down = merged(sizes, lambda step: max(step) <= 0)
        self.up = merged(sizes, lambda step: min(step) >= 0)
        self.first = lax.axis_index("gx") == 0
        steps = Z_STEPS + tuple(m[0] for m in self.messages + self.down + self.up)
        self.places = {step: neighbour(sizes, step) for step in steps}

    def remote(self, slot, number, step, source, target):
        return pltpu.make_async_remote_copy(
            src_ref=source,
            dst_ref=target,
            send_sem=self.send_sem.at[slot, number],
            recv_sem=self.recv_sem.at[slot, number],
            device_id=self.places[step],
            device_id_type=MESH,
        )

    def lines(self, cell, step):
        first = cell * CELL_ROWS
        if step[1] == 0:
            return [pl.ds(first + side_of(step[0]) * SIDE * TILE, SIDE * TILE)]
        if step[0] == 0:
            rows = range(SIDE)
        else:
            rows = [side_of(step[0])]
        return [pl.ds(first + (a * SIDE + side_of(step[1])) * TILE, TILE) for a in rows]

    def send_faces(self, slot, group, cells, messages):
        copies = []
        row = 0
        for n, steps in enumerate(messages):
            begin = row
            for step in steps:
                part = [self.work[at, :] for k in cells for at in self.lines(k, step)]
                size = part_rows(step, len(cells))
                self.f_send[slot, group, row : row + size, :] = jnp.concatenate(part, 0).astype(
                    self.f_send.dtype
                )
                row += size
            rows = pl.ds(begin, row - begin)
            copies.append(
                self.remote(
                    slot,
                    len(Z_STEPS) + group * len(self.messages) + n,
                    steps[0],
                    self.f_send.at[slot, group, rows],
                    self.f_recv.at[slot, group, rows],
                )
            )
            if n and steps[0][0] == -1 and messages[n - 1][0][0] == 1:
                self.start_pair(copies[-2], copies[-1])
            elif n + 1 == len(messages) or steps[0][0] != 1 or messages[n + 1][0][0] != -1:
                copies[-1].start()
        return copies

    def start_pair(self, upward, downward):
        @pl.when(self.first)
        def _():
            downward.start()
            upward.start()

        @pl.when(jnp.logical_not(self.first))
        def _():
            upward.start()
            downward.start()

    def add_faces(self, slot, group, cells, copies, messages):
        row = 0
        for copy, steps in zip(copies, messages):
            copy.wait()
            for step in steps:
                size = part_rows(step, len(cells))
                got = self.f_recv[slot, group, row : row + size, :].astype(jnp.float32)
                row += size
                taken = 0
                for k in cells:
                    for at in self.lines(k, tuple(-d for d in step)):
                        self.work[at, :] = self.work[at, :] + got[taken : taken + at.size]
                        taken += at.size

    def z_rows(self, cell, c):
        return pl.ds(cell * CELL_ROWS + c, LINES, stride=TILE)

    def z_copies(self, slot):
        return [
            self.remote(slot, n, step, self.z_send.at[slot, n], self.z_recv.at[slot, n])
            for n, step in enumerate(Z_STEPS)
        ]

    def send_z(self, slot):
        work = self.work
        self.z_send[slot, 0] = work[self.z_rows(self.cells - 1, ORDER), :]
        self.z_send[slot, 1] = work[self.z_rows(0, 0), :]
        for copy in self.z_copies(slot):
            copy.start()
        for cell in range(self.cells - 1):
            lower, upper = self.z_rows(cell, ORDER), self.z_rows(cell + 1, 0)
            both = work[lower, :] + work[upper, :]
            work[lower, :] = both
            work[upper, :] = both

    def add_z(self, slot):
        work = self.work
        for copy in self.z_copies(slot):
            copy.wait()
        bottom, top = self.z_rows(0, 0), self.z_rows(self.cells - 1, ORDER)
        work[bottom, :] = work[bottom, :] + self.z_recv[slot, 0]
        work[top, :] = work[top, :] + self.z_recv[slot, 1]


def inverse_factor(gram, mixed, inverse):
    n = gram.shape[0]
    size = BLOCK_ROWS if n % BLOCK_ROWS == 0 else TILE
    mixed[...] = gram
    sub = lax.broadcasted_iota(jnp.int32, (size, n), 0)
    col = lax.broadcasted_iota(jnp.int32, (size, n), 1)
    for start in range(0, n, size):
        end = start + size
        rows = mixed[start:end, :]
        cols = [jnp.broadcast_to(rows[:, start + t : start + t + 1], (size, n)) for t in range(size)]
        unit = jnp.where(col - start == sub, 1.0, 0.0).astype(jnp.float32)
        rows = jnp.where((col >= start) & (col < end), unit, rows)
        scale = jnp.zeros((size, n), jnp.float32)
        for s in range(size):
            root = lax.rsqrt(cols[s][s : s + 1, :])
            scale = jnp.where(sub == s, root, scale)
            if s + 1 < size:
                ratio = jnp.where(sub > s, cols[s] * (root * root), 0.0)
                for t in range(s + 1, size):
                    cols[t] = cols[t] - ratio * cols[t][s : s + 1, :]
                rows = rows - ratio * rows[s : s + 1, :]
        rows = rows * scale
        inverse[start:end, :] = jnp.where(col < end, rows, 0.0)
        if end < n:
            change = dot_rows(jnp.where(col >= end, rows, 0.0), rows, HIGHEST)[end:, :]
            rest = lax.broadcasted_iota(jnp.int32, (n - end, n), 1)
            kept = jnp.where((rest >= start) & (rest < end), 0.0, mixed[end:, :])
            mixed[end:, :] = kept - change


def kernel(
    sizes,
    cells,
    nodes_total,
    coef_ref,
    start_ref,
    locked_ref,
    h_ref,
    parts,
    gram_rows,
    padded_h,
    grid_nodes,
    state,
    work,
    z_send,
    z_recv,
    f_send,
    f_recv,
    halo_sems,
    locked_t,
    cross_part,
    cross_scratch,
    coefficient,
    gram_part,
    gram_scratch,
):
    width = work.shape[1]
    node = h_ref.shape[1]
    steps = greeted(sizes, [groups(sizes, locked_ref.shape[1])[0], groups(sizes, width)[0], *[(a,) for a in AXES]])
    barrier = pltpu.get_barrier_semaphore()
    for step in steps:
        pl.semaphore_signal(
            barrier, inc=1, device_id=neighbour(sizes, step), device_id_type=MESH
        )

    own = start_ref.shape[2]
    grid_nodes[...] = jnp.zeros_like(grid_nodes)
    grid_nodes[:, :, :own, :] = start_ref[...].astype(jnp.float32)
    work[...] = jnp.zeros_like(work)
    sub = lax.broadcasted_iota(jnp.int32, (ORDER, TILE, width), 1)
    for k in range(cells):
        for a in range(ORDER):
            values = grid_nodes[a, :, ORDER * k : ORDER * k + TILE, :]
            first = k * CELL_ROWS + a * SIDE * TILE
            work[first : first + ORDER * TILE, :] = jnp.where(sub < ORDER, values, 0.0).reshape(
                ORDER * TILE, width
            )
    pl.semaphore_wait(barrier, len(steps))
    halo = Halo(sizes, cells, work, z_send, z_recv, f_send, f_recv, halo_sems)
    inner, outer = tuple(range(1, cells - 1)), (0, cells - 1)
    state[...] = jnp.zeros(state.shape, jnp.float32)

    def finish_faces(slot, inner_copies, outer_copies, messages):
        halo.add_faces(slot, 0, inner, inner_copies, messages)
        halo.add_faces(slot, 1, outer, outer_copies, messages)
        halo.send_z(slot)

    def update(t, group):
        now, old = lax.rem(t, 2), lax.rem(t + 1, 2)
        scale, shift, back = coef_ref[t, 0], coef_ref[t, 1], coef_ref[t, 2]
        for k in group:
            rows = pl.ds(k * CELL_ROWS, CELL_ROWS)
            state[now, rows, :] = (
                scale * (work[rows, :] - shift * state[old, rows, :]) - back * state[now, rows, :]
            )

    def multiply(t, group):
        for k in group:
            rows = pl.ds(k * CELL_ROWS, CELL_ROWS)
            values = state[lax.rem(t, 2), rows, :].astype(jnp.bfloat16)
            work[rows, :] = jnp.dot(padded_h[k], values, preferred_element_type=jnp.float32)

    inner_copies = halo.send_faces(0, 0, inner, halo.down)
    outer_copies = halo.send_faces(0, 1, outer, halo.down)
    row = lax.broadcasted_iota(jnp.int32, (CELL_ROWS, node), 0)
    col = lax.broadcasted_iota(jnp.int32, (CELL_ROWS, node), 1)
    place = jnp.where(row % TILE < SIDE, row // TILE * SIDE + row % TILE, -1)
    spread = jnp.where(col == place, 1.0, 0.0).astype(jnp.bfloat16)
    for k in range(cells):
        tall = jnp.dot(spread, h_ref[k], preferred_element_type=jnp.float32).astype(jnp.bfloat16)
        padded_h[k] = lax.dot_general(
            tall, spread, (((1,), (1,)), ((), ())), preferred_element_type=jnp.float32
        ).astype(jnp.bfloat16)
    locked_t[...] = locked_ref[...].T
    finish_faces(0, inner_copies, outer_copies, halo.down)

    def apply(t, messages):
        slot = lax.rem(t, 2)
        update(t - 1, inner)
        multiply(t - 1, inner)
        inner_copies = halo.send_faces(slot, 0, inner, messages)
        halo.add_z(lax.rem(t - 1, 2))
        update(t - 1, outer)
        multiply(t - 1, outer)
        outer_copies = halo.send_faces(slot, 1, outer, messages)
        finish_faces(slot, inner_copies, outer_copies, messages)

    def repeat(t, carry):
        apply(t, halo.messages)
        return carry

    lax.fori_loop(1, APPLY, repeat, 0)
    apply(APPLY, halo.up)
    update(APPLY, inner)
    halo.add_z(APPLY % 2)
    update(APPLY, outer)
    last = APPLY % 2
    for k in range(cells):
        for a in range(ORDER):
            first = k * CELL_ROWS + a * SIDE * TILE
            grid_nodes[a, :, ORDER * k : ORDER * k + TILE, :] = state[
                last, first : first + ORDER * TILE, :
            ].reshape(ORDER, TILE, width)
    filtered = (
        grid_nodes[:, :, :own, :].reshape(ORDER * ORDER * own, width).astype(jnp.bfloat16)
    )
    cross_part[...] = jnp.dot(
        locked_t[...], filtered, preferred_element_type=jnp.float32
    ).astype(cross_part.dtype)
    sum_over_devices(
        sizes,
        cross_part,
        cross_scratch,
        lambda total: (total / nodes_total).astype(jnp.bfloat16),
        coefficient,
    )
    projected = filtered.astype(jnp.float32) - jnp.dot(
        locked_ref[...],
        coefficient[...].reshape(locked_ref.shape[1], width),
        preferred_element_type=jnp.float32,
    )
    high, low = split(projected)
    parts[:, :width] = high
    parts[:, width:] = low
    terms = dot_rows(parts[...], parts[...])
    gram_part[...] = (
        terms[:width, :width]
        + (terms[:width, width:] + terms[width:, :width])
        + terms[width:, width:]
    )
    sum_over_devices(sizes, gram_part, gram_scratch, lambda total: total / nodes_total, gram_rows)


def finish_kernel(parts, gram_rows, out_ref, mixed, inverse):
    width = out_ref.shape[1]
    inverse_factor(gram_rows[...].reshape(width, width), mixed, inverse)
    inverse_high, inverse_low = split(inverse[...])
    wide = jnp.concatenate([inverse_high, inverse_high], axis=1)
    contract = (((1,), (1,)), ((), ()))
    out_ref[...] = lax.dot_general(
        parts[...], wide, contract, preferred_element_type=jnp.float32
    ) + lax.dot_general(
        parts[:, :width], inverse_low, contract, preferred_element_type=jnp.float32
    )


def per_device(sizes, start_block, locked_orbitals, cell_h):
    width = start_block.shape[3]
    locked = locked_orbitals.shape[3]
    own = start_block.shape[2]
    cells = cell_h.shape[2]
    assert cell_h.shape[:2] == (1, 1)
    nodes = ORDER * ORDER * own
    nodes_total = float(nodes * count_of(sizes, AXES))
    count = lambda rows: count_of(sizes, groups(sizes, rows)[0])
    largest = max(cells - 2, 2)
    faces = sum(part_rows(step, largest) for step in X_STEPS + Y_STEPS + XY_STEPS)
    messages = len(Z_STEPS) + 2 * len(merged(sizes))
    vmem = pltpu.VMEM
    scratch = [
        vmem((cells, CELL_ROWS, CELL_ROWS), jnp.bfloat16),
        vmem((ORDER, ORDER, own + TILE, width), jnp.float32),
        vmem((2, cells * CELL_ROWS, width), jnp.float32),
        vmem((cells * CELL_ROWS, width), jnp.float32),
        vmem((2, 2, LINES, width), jnp.float32),
        vmem((2, 2, LINES, width), jnp.float32),
        vmem((2, 2, faces, width), jnp.bfloat16),
        vmem((2, 2, faces, width), jnp.bfloat16),
        [pltpu.SemaphoreType.DMA((2, messages))] * 2,
        vmem((locked, nodes), jnp.bfloat16),
        vmem((locked, width), jnp.bfloat16),
        sum_scratch(sizes, locked, width, jnp.bfloat16),
        vmem((count(locked), locked // count(locked), width), jnp.bfloat16),
        vmem((width, width), jnp.float32),
        sum_scratch(sizes, width, width),
    ]
    block = pl.BlockSpec(memory_space=pltpu.VMEM)
    parts, gram = pl.pallas_call(
        functools.partial(kernel, sizes, cells, nodes_total),
        out_shape=(
            jax.ShapeDtypeStruct((nodes, 2 * width), jnp.bfloat16),
            jax.ShapeDtypeStruct((count(width), width // count(width), width), jnp.float32),
        ),
        in_specs=[pl.BlockSpec(memory_space=pltpu.SMEM)]
        + [block] * 3,
        out_specs=(block, block),
        scratch_shapes=scratch,
        compiler_params=pltpu.CompilerParams(
            collective_id=0, has_side_effects=True, vmem_limit_bytes=40 << 20
        ),
    )(
        jnp.asarray(recurrence()),
        start_block,
        locked_orbitals.reshape(nodes, locked),
        cell_h.reshape(cell_h.shape[2:]),
    )
    result = pl.pallas_call(
        finish_kernel,
        out_shape=jax.ShapeDtypeStruct((nodes, width), jnp.float32),
        in_specs=[block, block],
        out_specs=block,
        scratch_shapes=[vmem((width, width), jnp.float32), vmem((width, width), jnp.float32)],
        compiler_params=pltpu.CompilerParams(vmem_limit_bytes=16 << 20),
    )(parts, gram)
    return result.reshape(start_block.shape)


def solution(mesh):
    sizes = dict(mesh.shape)
    placed = (P("gx", "gy", "gz", None), P("gx", "gy", "gz", None), P("gx", "gy", "gz", None, None))
    return jax.shard_map(
        functools.partial(per_device, sizes),
        mesh=mesh,
        in_specs=placed,
        out_specs=P("gx", "gy", "gz", None),
        check_vma=False,
    )
```
